128 devices in a mesh: occ: 8 (over y_hi, x), vir: 16 (over z, y_lo, core).
Axes of the slice: x: 4, y: 4 (y_hi: 2, y_lo: 2; y = y_hi * 2 + y_lo), z: 4, core: 2. Of those that a mesh axis runs over, the one named last changes fastest.
Arguments:
- amplitudes: float32 [4, 32, 128, 128], P(None, 'occ', 'vir'), may hold values from -6 to 6
- vv_factors: float32 [768, 128, 128], P('occ', 'vir'), may hold values from -0.3 to 0.3
- ov_factors: float32 [768, 32, 128], P(None, 'occ', 'vir'), may hold values from -0.3 to 0.3
- occ_irreps: int32 [32], replicated, may hold values from 0 to 7
- vir_irreps: int32 [128], replicated, may hold values from 0 to 7
- aux_irreps: int32 [768], replicated, may hold values from 0 to 7
Outputs:
- residual: float32 [4, 32, 128, 128], P(None, 'occ', 'vir')
The draws below stay inside these ranges and needn't reach their ends.
Inputs may be any that keep to these rules, and one draw needn't show every extreme that they name: `vir_irreps`: irrep labels of the point group D2h.
All inputs are finite; a program needn't handle non-finite values.
Results may differ from the reference program's by a relative error of at most 0.000086.
Values sent between devices are 32-bit elements; how exact they have to be, the bound alone decides.
No kernel may reach another device: no remote copies, remote signals or barrier semaphores. Data moves between devices by JAX's collectives and lax.ppermute only.
A program may use at most 192 MiB of HBM per device.

```python
import jax
import jax.numpy as jnp
from jax import lax

O = 32
V = 128
NAUX = 768
IW = 4


def set_ends(values, own_key, low, high):
    spot = [jax.random.randint(jax.random.fold_in(own_key, axis), (), 0, length) for axis, length in enumerate(values.shape)]
    main_axis = values.shape.index(max(values.shape))
    beside = spot[:main_axis] + [(spot[main_axis] + 1) % values.shape[main_axis]] + spot[main_axis + 1:]
    return values.at[tuple(spot)].set(low).at[tuple(beside)].set(high)


def block_levels(own_key, shape, shards, low, high):
    gain = 1.0
    for axis_at, shards_of in shards:
        draws = jax.random.uniform(jax.random.fold_in(jax.random.fold_in(own_key, 6), axis_at), (shards_of,), jnp.float32, low / len(shards), high / len(shards))
        gain = gain * jnp.repeat(jnp.exp(draws), shape[axis_at] // shards_of).reshape((-1,) + (1,) * (len(shape) - 1 - axis_at))
    return gain


def noise(key, dims, width, limit, shards=(), held_as=jnp.bfloat16):
    array = width * jax.random.normal(key, dims, jnp.float32)
    if shards:
        array = array * block_levels(key, dims, shards, -0.22, 0.18)
    return jnp.clip(array, -limit, limit).astype(held_as)


def setup_inputs(seed: int = 0) -> dict:
    key_list = jax.random.split(jax.random.key(seed), 7)
    return {
        "amplitudes": noise(key_list[0], (IW, O, V, V), 1.0, 6.0, ((1, 8), (2, 16)), jnp.float32),
        "vv_factors": noise(key_list[1], (NAUX, V, V), 0.05, 0.3, ((0, 8), (1, 16)), jnp.float32),
        "ov_factors": noise(key_list[2], (NAUX, O, V), 0.05, 0.3, ((1, 8), (2, 16)), jnp.float32),
        "occ_irreps": set_ends(jax.random.randint(key_list[3], (O,), 0, 8), jax.random.fold_in(key_list[3], 1), 0, 7).astype(jnp.int32),
        "vir_irreps": set_ends(jax.random.randint(key_list[4], (V,), 0, 8), jax.random.fold_in(key_list[4], 1), 0, 7).astype(jnp.int32),
        "aux_irreps": set_ends(jax.random.randint(key_list[5], (NAUX,), 0, 8), jax.random.fold_in(key_list[5], 1), 0, 7).astype(jnp.int32),
    }


def allowed(left, right, target):
    return (jnp.bitwise_xor(left, right) == target).astype(jnp.float32)


def reference(amplitudes, vv_factors, ov_factors, occ_irreps, vir_irreps, aux_irreps):
    high = lax.Precision.HIGHEST
    vv_masked = vv_factors * allowed(vir_irreps[None, :, None], vir_irreps[None, None, :], aux_irreps[:, None, None])
    ov_masked = ov_factors * allowed(occ_irreps[None, :, None], vir_irreps[None, None, :], aux_irreps[:, None, None])

    def per_virtual(factor_row):
        inter = jnp.einsum("qc,qbd->cbd", factor_row, vv_masked, precision=high)
        return jnp.einsum("ijcd,cbd->ijb", amplitudes, inter, precision=high)

    stacked = lax.map(per_virtual, jnp.moveaxis(vv_masked, 1, 0))
    ladder = jnp.transpose(stacked, (1, 2, 0, 3))
    cycle_amps = 2.0 * amplitudes - jnp.transpose(amplitudes, (0, 1, 3, 2))
    factor = jnp.einsum("ikac,qkc->iaq", cycle_amps, ov_masked, precision=high)
    cycle = jnp.einsum("iaq,qjb->ijab", factor, ov_masked, precision=high)
    return ladder + cycle
```

```python
import functools

import jax
import jax.numpy as jnp
from jax import lax
from jax.experimental import pallas as pl
from jax.experimental.pallas import tpu as pltpu
from jax.sharding import Mesh, PartitionSpec as P

OCC = ("yh", "x")
ZY = ("z", "yl")
VIR = ("z", "yl", "core")
F32 = jnp.float32
BF16 = jnp.bfloat16
HIGHEST = lax.Precision.HIGHEST
SL = 24
SG = 128
NG = 8
VMEM = pl.BlockSpec(memory_space=pltpu.VMEM)
SMEM = pl.BlockSpec(memory_space=pltpu.SMEM)
LIMIT = 56 * 2**20


def occ_at():
    return lax.axis_index("yh") * 4 + lax.axis_index("x")


def vir_at():
    return lax.axis_index("z") * 4 + lax.axis_index("yl") * 2 + lax.axis_index("core")


def iota(shape, dim):
    return lax.broadcasted_iota(jnp.int32, shape, dim)


def split(x):
    hi = x.astype(BF16)
    return hi, (x - hi.astype(F32)).astype(BF16)


def dot(x, y):
    return jnp.dot(x, y, preferred_element_type=F32)


def dot_t(x, y, precision=None):
    return lax.dot_general(x, y, (((1,), (1,)), ((), ())), precision=precision, preferred_element_type=F32)


def call(body, outs, n_smem, n_vmem, scratch=(), cost=(0, 0)):
    return pl.pallas_call(
        body,
        out_shape=outs,
        in_specs=[SMEM] * n_smem + [VMEM] * n_vmem,
        out_specs=jax.tree.map(lambda _: VMEM, outs),
        scratch_shapes=list(scratch),
        compiler_params=pltpu.CompilerParams(vmem_limit_bytes=LIMIT),
        cost_estimate=pl.CostEstimate(flops=cost[0], bytes_accessed=cost[1], transcendentals=0),
    )


def fold_local(vir_s, lab_ref, b_ref, t_ref, out_ref, roll_ref):
    o, v = occ_at(), vir_at()
    q_lane = jnp.broadcast_to(lab_ref[pl.ds(o, 1), :], (128, 128))
    q_sub = jnp.transpose(q_lane)
    same = (q_sub == q_lane) & (iota((128, 128), 0) < iota((128, 128), 1))
    rank = jnp.sum(same.astype(F32), axis=0, keepdims=True)
    pick = (rank == iota((SL, 128), 0).astype(F32)).astype(F32)[:, :96].astype(BF16)
    y_row = lab_ref[8:9, :]
    for x in range(8):
        keep = (y_row ^ vir_s[v * 8 + x]) == q_sub[:96]
        hi, lo = split(jnp.where(keep, b_ref[:, x, :], 0.0))
        folded = dot(pick, hi) + dot(pick, lo)
        for peer in range(8):
            out_ref[peer, x * SL : (x + 1) * SL, :] = folded
    amps = t_ref[...].reshape(16, 8, 128)
    for k in range(8):
        roll_ref[k] = pltpu.roll(amps, 16 * k, 2) if k else amps
    group = iota((16, 128), 1) // 16
    for peer in range(8):
        block = jnp.zeros((16, 128), F32)
        for c in range(8):
            block = jnp.where(group == c, roll_ref[(c - peer) % 8, :, c, :], block)
        out_ref[peer, 8 * SL : 8 * SL + 16, :] = block


def fold_ov(vir_s, occ_s, aux_ref, c_ref, t_ref, ch_ref, sw_ref):
    o, v = occ_at(), vir_at()
    aux = aux_ref[...]
    member = (aux == iota((NG, 768), 0)).astype(F32)
    before = (iota((768, 768), 0) < iota((768, 768), 1)).astype(F32).astype(BF16)
    rank = jnp.sum(member * dot(member.astype(BF16), before), axis=0, keepdims=True)
    pick = (rank == iota((SG, 768), 0).astype(F32)).astype(F32).astype(BF16)
    c_label = jnp.zeros((8, 1), jnp.int32)
    for c in range(8):
        c_label = jnp.where(iota((8, 1), 0) == c, vir_s[v * 8 + c], c_label)
    for k in range(4):
        keep = (c_label ^ occ_s[o * 4 + k]) == aux
        hi, lo = split(jnp.where(keep, c_ref[k], 0.0))
        ch_ref[8 * k : 8 * k + 8, :] = dot_t(hi, pick) + dot_t(lo, pick)
    sw_ref[...] = jnp.transpose(t_ref[...].reshape(128, 128))


def place(lab_ref, place_ref):
    lane = iota((SL, 128), 1).astype(F32) - iota((SL, 128), 0).astype(F32)
    aux = lab_ref[0:8, :]
    for g in range(NG):
        count = jnp.sum((aux == g).astype(F32), axis=1, keepdims=True)
        start = jnp.zeros((1, 1), F32)
        for block in range(8):
            row = g * 256 + block * SL
            place_ref[row : row + SL, :] = (lane == start).astype(F32)
            start = start + count[block : block + 1, :]
        place_ref[g * 256 + 8 * SL : (g + 1) * 256, :] = jnp.zeros((256 - 8 * SL, 128), F32)


def refold_own(vir_s, lab_ref, r1_ref, ch_ref, sw_ref, out_ref, place_ref, row_ref):
    o, v = occ_at(), vir_at()
    place(lab_ref, place_ref)
    group = iota((1, 128), 1) // 16
    y_row = jnp.broadcast_to(lab_ref[8:9, :], (8, 128))
    mine = jnp.zeros((8 * SL, 128), F32)
    label = jnp.zeros((8, 128), jnp.int32)
    for x in range(8):
        shift = lax.rem(16 * x + 128 - 16 * o, 128)
        block = jnp.concatenate([r1_ref[p, x * SL : (x + 1) * SL, :] for p in range(8)], axis=0)
        mine = jnp.where(group == x, pltpu.roll(block, shift, 1), mine)
        label = jnp.where(group == x, pltpu.roll(y_row, shift, 1) ^ vir_s[v * 8 + x], label)
    mine = jnp.transpose(jnp.concatenate([mine, jnp.zeros((256 - 8 * SL, 128), F32)], axis=0))
    label = jnp.transpose(jnp.broadcast_to(label[0:1], (128, 128)))
    label = jnp.concatenate([label, label], axis=1)
    hi, lo = split(mine)
    hi, lo = hi.astype(F32), lo.astype(F32)
    total = jnp.zeros((256, 128), F32)
    for g in range(NG):
        both = jnp.concatenate([jnp.where(label == g, hi, 0.0), jnp.where(label == g, lo, 0.0)], axis=0)
        total = total + dot(both.astype(BF16), place_ref[g * 256 : (g + 1) * 256, :].astype(BF16))
    row_ref[0] = total[:128] + total[128:]
    row_ref[1] = jnp.transpose(
        jnp.concatenate([r1_ref[p, 8 * SL : 8 * SL + 16, :] for p in range(8)], axis=0)
    )
    for d in range(16):
        own = row_ref[0, pl.ds(d, 8, stride=16), :]
        amps = row_ref[1, pl.ds(d, 8, stride=16), :]
        for peer in range(8):
            out_ref[peer, d * 8 : d * 8 + 8, :] = own
            out_ref[peer, 128 + d * 8 : 136 + d * 8, :] = amps
    for peer in range(8):
        out_ref[peer, 256:288, :] = ch_ref[...]
        out_ref[peer, 288:304, :] = sw_ref[16 * peer : 16 * peer + 16, :]


def refold_rows(vir_s, lab_ref, r1_ref, out_ref, place_ref):
    v = vir_at()
    place(lab_ref, place_ref)
    spread = jnp.concatenate(
        [jnp.transpose(place_ref[128 * n : 128 * n + 128, :]).astype(BF16) for n in range(2 * NG)], axis=1
    )
    y_row = lab_ref[8:9, :]
    pad = jnp.zeros((256 - 8 * SL, 128), F32)
    for x in range(8):
        label = y_row ^ vir_s[v * 8 + x]
        block = jnp.concatenate([r1_ref[p, x * SL : (x + 1) * SL, :] for p in range(8)] + [pad], axis=0)
        hi, lo = split(block)
        both = jnp.concatenate([hi, lo], axis=1)
        total = jnp.zeros((SG, 256), F32)
        for g in range(NG):
            keep = (label == g).astype(F32)
            keep = jnp.concatenate([keep, keep], axis=1).astype(BF16)
            total = total + dot(spread[:, g * 256 : (g + 1) * 256], both * keep)
        hi, lo = split(total[:, :128] + total[:, 128:])
        out_ref[0:128, x * 128 : x * 128 + 128] = hi
        out_ref[128:256, x * 128 : x * 128 + 128] = lo
        out_ref[256:384, x * 128 : x * 128 + 128] = hi


def cycle_first(occ_s, lab_ref, r2_ref, o2_ref, t_ref, y_ref, chat_ref, got_ref):
    o, core = occ_at(), lax.axis_index("core")
    for p in range(8):
        got_ref[2 * p + core] = r2_ref[p, 256:304, :]
        got_ref[2 * p + 1 - core] = o2_ref[p, 256:304, :]
    for k in range(4):
        for n in range(16):
            chat_ref[k * 128 + n * 8 : k * 128 + n * 8 + 8, :] = got_ref[n, 8 * k : 8 * k + 8, :]
    group = iota((8, 128), 1) // 8
    blocks = [got_ref[n, pl.ds(pl.multiple_of(32 + 8 * core, 8), 8), :] for n in range(16)]
    u = []
    for i in range(4):
        row = []
        for k in range(4):
            swapped = jnp.zeros((8, 128), F32)
            for n in range(16):
                shift = (8 * (n - 4 * i - k)) % 128
                swapped = jnp.where(group == n, pltpu.roll(blocks[n], shift, 1) if shift else blocks[n], swapped)
            row.append(2.0 * t_ref[i, k] - swapped)
        u.append(jnp.concatenate(row, axis=1))
    u = jnp.concatenate(u, axis=0)
    label = jnp.concatenate([lab_ref[8:9, :] ^ occ_s[o * 4 + k] for k in range(4)], axis=1)
    rows = jnp.concatenate([jnp.where(label == g, u, 0.0) for g in range(NG)], axis=0)
    y = jnp.dot(rows, chat_ref[...], precision=HIGHEST, preferred_element_type=F32)
    for peer in range(8):
        y_ref[peer] = y


def ladder(vir_s, lab_ref, b1_ref, r2_ref, o2_ref, out_ref, f_ref, t_ref, hi_ref, lo_ref, acc_ref):
    o, v, core = occ_at(), vir_at(), lax.axis_index("core")
    for ref, part in ((r2_ref, core), (o2_ref, 1 - core)):
        for p in range(8):
            f_ref[:, 2 * p + part] = ref[p, 0:128, :].reshape(16, 8, 128)
            t_ref[:, 2 * p + part] = ref[p, 128:256, :].reshape(16, 8, 128)
    acc_ref[...] = jnp.zeros_like(acc_ref)
    c_lane = jnp.broadcast_to(lab_ref[8:9, :], (128, 128))
    bc = jnp.transpose(c_lane) ^ c_lane

    def step(n, carry):
        amps = []
        for half in range(2):
            d = 2 * n + half
            hi, lo = split(f_ref[d].reshape(128, 128))
            w = dot(jnp.concatenate([hi, hi, lo], axis=1), b1_ref[...])
            d_label = vir_s[o * 16 + d]
            for a in range(8):
                keep = bc == (vir_s[v * 8 + a] ^ d_label)
                hi, lo = split(jnp.where(keep, w[:, a * 128 : a * 128 + 128], 0.0))
                hi_ref[a * 128 : a * 128 + 128, half * 128 : half * 128 + 128] = hi
                lo_ref[a * 128 : a * 128 + 128, half * 128 : half * 128 + 128] = lo
            amps.append(t_ref[d].reshape(128, 128))
        hi, lo = split(jnp.concatenate(amps, axis=0))
        r = dot(hi_ref[...], jnp.concatenate([hi, lo], axis=1))
        acc_ref[...] += r[:, :128] + r[:, 128:] + dot(lo_ref[...], hi)
        return carry

    lax.fori_loop(0, 8, step, 0)
    for a in range(8):
        rows = jnp.transpose(acc_ref[a * 128 : a * 128 + 128, :])
        for p in range(8):
            out_ref[p, a] = rows[16 * p : 16 * p + 16, :]


def finish(occ_s, lab_ref, r3_ref, y_ref, chat_ref, out_ref, sum_ref):
    o = occ_at()
    total = r3_ref[0]
    y = y_ref[0]
    for p in range(1, 8):
        total = total + r3_ref[p]
        y = y + y_ref[p]
    sum_ref[...] = total
    z = dot_t(y, chat_ref[...], HIGHEST)
    for j in range(4):
        label = lab_ref[8:9, :] ^ occ_s[o * 4 + j]
        part = jnp.zeros((32, 128), F32)
        for g in range(NG):
            part = jnp.where(label == g, z[g * 32 : g * 32 + 32, j * 128 : j * 128 + 128], part)
        for i in range(4):
            out_ref[i, j] = sum_ref[:, i * 4 + j, :] + part[8 * i : 8 * i + 8, :]


def swap(x, axes):
    return lax.all_to_all(x, axes, 0, 0, tiled=True)


def folded(t, b, c, occ, vir, aux):
    aux8 = jnp.pad(aux.reshape(8, 96), ((0, 0), (0, 32)), constant_values=NG)
    rest = jnp.stack([vir, jnp.pad(occ, (0, 96), constant_values=NG)])
    lab = jnp.concatenate([aux8, rest, jnp.zeros((6, 128), jnp.int32)], axis=0)
    shape = jax.ShapeDtypeStruct
    p1 = call(
        fold_local, shape((8, 8 * SL + 16, 128), F32), 1, 3, [pltpu.VMEM((8, 16, 8, 128), F32)],
        (2 * 2 * 24 * 96 * 1024, 1300000),
    )(vir, lab, b, t)
    r1 = swap(p1, OCC)
    ch, sw = call(
        fold_ov, (shape((32, 128), F32), shape((128, 128), F32)), 2, 3, (), (2 * 8 * 768 * 768 + 4 * 32 * 768 * 128, 300000)
    )(vir, occ, aux.reshape(1, 768), jnp.transpose(c, (1, 2, 0)), t)
    p2 = call(
        refold_own, shape((8, 304, 128), F32), 1, 4, [pltpu.VMEM((2048, 128), F32), pltpu.VMEM((2, 128, 128), F32)],
        (2 * 256 * 2048 * 128, 2300000),
    )(vir, lab, r1, ch, sw)
    r2 = swap(p2, ZY)
    b1 = call(
        refold_rows, shape((384, 1024), BF16), 1, 2, [pltpu.VMEM((2048, 128), F32)], (2 * 128 * 2048 * 2048, 1700000)
    )(vir, lab, r1)
    o2 = lax.ppermute(r2, "core", [(0, 1), (1, 0)])
    yp, chat = call(
        cycle_first, (shape((8, 256, 128), F32), shape((512, 128), F32)), 1, 4, [pltpu.VMEM((16, 48, 128), F32)],
        (6 * 2 * 256 * 512 * 128, 4000000),
    )(occ, lab, r2, o2, t)
    yr = swap(yp, OCC)
    p3 = call(
        ladder, shape((8, 8, 16, 128), F32), 1, 4,
        [
            pltpu.VMEM((16, 16, 8, 128), F32),
            pltpu.VMEM((16, 16, 8, 128), F32),
            pltpu.VMEM((1024, 256), BF16),
            pltpu.VMEM((1024, 256), BF16),
            pltpu.VMEM((1024, 128), F32),
        ],
        (6 * 2048 * 1024 * 256, 4000000),
    )(vir, lab, b1, r2, o2)
    r3 = swap(p3, OCC)
    return call(
        finish, shape((4, 4, 8, 128), F32), 1, 4, [pltpu.VMEM((8, 16, 128), F32)], (6 * 2 * 256 * 512 * 128, 2000000)
    )(occ, lab, r3, yr, chat)


def allowed(left, right, target):
    return (jnp.bitwise_xor(left, right) == target).astype(F32)


def dense(t, b, c, occ, vir, aux):
    o, v = occ_at(), vir_at()
    aux_mine = lax.dynamic_slice_in_dim(aux, o * 96, 96)
    vir_mine = lax.dynamic_slice_in_dim(vir, v * 8, 8)
    occ_mine = lax.dynamic_slice_in_dim(occ, o * 4, 4)
    own = b * allowed(vir_mine[None, :, None], vir[None, None, :], aux_mine[:, None, None])
    wide = lax.all_gather(b, VIR, axis=1, tiled=True)
    wide = wide * allowed(vir[None, :, None], vir[None, None, :], aux_mine[:, None, None])
    pairs = lax.all_gather(t, OCC, axis=1, tiled=True)
    inter = jnp.einsum("qac,qbd->acbd", own, wide, precision=HIGHEST)
    part = jnp.einsum("ijcd,acbd->ijab", lax.all_gather(pairs, VIR, axis=2, tiled=True), inter, precision=HIGHEST)
    total = lax.psum_scatter(part, OCC, scatter_dimension=1, tiled=True)
    swapped = lax.all_to_all(t, VIR, split_axis=3, concat_axis=2, tiled=True)
    u = 2.0 * t - jnp.transpose(swapped, (0, 1, 3, 2))
    cw = lax.all_gather(c, VIR, axis=2, tiled=True)
    cw = cw * allowed(occ_mine[None, :, None], vir[None, None, :], aux[:, None, None])
    y = lax.psum(jnp.einsum("ikac,qkc->iaq", u, cw, precision=HIGHEST), OCC)
    return total + jnp.einsum("iaq,qjb->ijab", y, cw, precision=HIGHEST)


def shards(t, b, c, occ, vir, aux):
    fast = folded(t, b, c, occ, vir, aux)
    member = aux.reshape(1, 8, 96) == jnp.arange(NG, dtype=jnp.int32).reshape(NG, 1, 1)
    count = jnp.sum(member.astype(jnp.int32), axis=2)
    fits = (jnp.max(count) <= SL) & (jnp.max(jnp.sum(count, axis=1)) <= SG)
    return lax.cond(fits, lambda *_: fast, dense, t, b, c, occ, vir, aux)


def solution(mesh):
    fine = Mesh(mesh.devices.reshape(2, 4, 4, 2, 2), ("yh", "x", "z", "yl", "core"))
    placed = (P(None, OCC, VIR, None), P(OCC, VIR, None), P(None, OCC, VIR), P(), P(), P())
    return jax.shard_map(shards, mesh=fine, in_specs=placed, out_specs=P(None, OCC, VIR, None), check_vma=False)
```

```python
import functools

import jax
import jax.numpy as jnp
from jax import lax
from jax.experimental import pallas as pl
from jax.experimental.pallas import tpu as pltpu
from jax.sharding import Mesh, PartitionSpec as P

OCC = ("yh", "x")
ZY = ("z", "yl")
VIR = ("z", "yl", "core")
F32 = jnp.float32
BF16 = jnp.bfloat16
HIGHEST = lax.Precision.HIGHEST
SL = 24
SG = 128
NG = 8
VMEM = pl.BlockSpec(memory_space=pltpu.VMEM)
SMEM = pl.BlockSpec(memory_space=pltpu.SMEM)
LIMIT = 14 * 2**20


def occ_at():
    return lax.axis_index("yh") * 4 + lax.axis_index("x")


def vir_at():
    return lax.axis_index("z") * 4 + lax.axis_index("yl") * 2 + lax.axis_index("core")


def iota(shape, dim):
    return lax.broadcasted_iota(jnp.int32, shape, dim)


def split(x):
    hi = x.astype(BF16)
    return hi, (x - hi.astype(F32)).astype(BF16)


def dot(x, y):
    return jnp.dot(x, y, preferred_element_type=F32)


def dot_t(x, y, precision=None):
    return lax.dot_general(x, y, (((1,), (1,)), ((), ())), precision=precision, preferred_element_type=F32)


def call(body, outs, n_smem, n_vmem, scratch=(), cost=(0, 0)):
    return pl.pallas_call(
        body,
        out_shape=outs,
        in_specs=[SMEM] * n_smem + [VMEM] * n_vmem,
        out_specs=jax.tree.map(lambda _: VMEM, outs),
        scratch_shapes=list(scratch),
        compiler_params=pltpu.CompilerParams(vmem_limit_bytes=LIMIT),
        cost_estimate=pl.CostEstimate(flops=cost[0], bytes_accessed=cost[1], transcendentals=0),
    )


def aux_block(aux_ref, block):
    row, skip = lax.div(3 * block, 4), 32 * lax.rem(3 * block, 4)
    first = jnp.broadcast_to(aux_ref[pl.ds(row, 1), :], (8, 128))
    second = jnp.broadcast_to(aux_ref[pl.ds(jnp.minimum(row + 1, 5), 1), :], (8, 128))
    lane = iota((8, 128), 1)
    shift = lax.rem(128 - skip, 128)
    joined = jnp.where(lane < 128 - skip, pltpu.roll(first, shift, 1), pltpu.roll(second, shift, 1))
    return jnp.where(lane < 96, joined, NG)


def aux_blocks(aux_ref):
    rows = jnp.zeros((8, 128), jnp.int32)
    for block in range(8):
        rows = jnp.where(iota((8, 128), 0) == block, aux_block(aux_ref, jnp.int32(block)), rows)
    return rows


def fold_local(vir_s, aux_ref, vir_ref, b_ref, t_ref, out_ref, roll_ref):
    o, v = occ_at(), vir_at()
    q_lane = jnp.broadcast_to(aux_block(aux_ref, o)[0:1], (128, 128))
    q_sub = jnp.transpose(q_lane)
    same = (q_sub == q_lane) & (iota((128, 128), 0) < iota((128, 128), 1))
    rank = jnp.sum(same.astype(F32), axis=0, keepdims=True)
    pick = (rank == iota((SL, 128), 0).astype(F32)).astype(F32)[:, :96].astype(BF16)
    y_row = vir_ref[...]
    for x in range(8):
        keep = (y_row ^ vir_s[v * 8 + x]) == q_sub[:96]
        hi, lo = split(jnp.where(keep, b_ref[:, x, :], 0.0))
        folded = dot(pick, hi) + dot(pick, lo)
        for peer in range(8):
            out_ref[peer, x * SL : (x + 1) * SL, :] = folded
    amps = t_ref[...].reshape(16, 8, 128)
    for k in range(8):
        roll_ref[k] = pltpu.roll(amps, 16 * k, 2) if k else amps
    group = iota((16, 128), 1) // 16
    for peer in range(8):
        block = jnp.zeros((16, 128), F32)
        for c in range(8):
            block = jnp.where(group == c, roll_ref[(c - peer) % 8, :, c, :], block)
        out_ref[peer, 8 * SL : 8 * SL + 16, :] = block


def fold_ov(vir_s, occ_s, aux_ref, c_ref, t_ref, ch_ref, sw_ref, fits_ref):
    o, v = occ_at(), vir_at()
    rows = aux_blocks(aux_ref)
    over = jnp.zeros((8, 1), F32)
    for g in range(NG):
        count = jnp.sum((rows == g).astype(F32), axis=1, keepdims=True)
        over = jnp.maximum(over, jnp.maximum(count - SL, jnp.sum(count, axis=0, keepdims=True) - SG))
    fits_ref[0] = (jnp.max(over) < 0.5).astype(jnp.int32)
    aux = jnp.concatenate([aux_ref[n : n + 1, :] for n in range(6)], axis=1)
    member = (aux == iota((NG, 768), 0)).astype(F32)
    before = (iota((768, 768), 0) < iota((768, 768), 1)).astype(F32).astype(BF16)
    rank = jnp.sum(member * dot(member.astype(BF16), before), axis=0, keepdims=True)
    pick = (rank == iota((SG, 768), 0).astype(F32)).astype(F32).astype(BF16)
    c_label = jnp.zeros((8, 1), jnp.int32)
    for c in range(8):
        c_label = jnp.where(iota((8, 1), 0) == c, vir_s[v * 8 + c], c_label)
    for k in range(4):
        keep = (c_label ^ occ_s[o * 4 + k]) == aux
        hi, lo = split(jnp.where(keep, c_ref[k], 0.0))
        ch_ref[8 * k : 8 * k + 8, :] = dot_t(hi, pick) + dot_t(lo, pick)
    sw_ref[...] = jnp.transpose(t_ref[...].reshape(128, 128))


def place(aux_ref, place_ref):
    lane = iota((SL, 128), 1).astype(F32) - iota((SL, 128), 0).astype(F32)
    aux = aux_blocks(aux_ref)
    for g in range(NG):
        count = jnp.sum((aux == g).astype(F32), axis=1, keepdims=True)
        start = jnp.zeros((1, 1), F32)
        for block in range(8):
            row = g * 256 + block * SL
            place_ref[row : row + SL, :] = (lane == start).astype(F32)
            start = start + count[block : block + 1, :]
        place_ref[g * 256 + 8 * SL : (g + 1) * 256, :] = jnp.zeros((256 - 8 * SL, 128), F32)


def refold_own(vir_s, aux_ref, vir_ref, r1_ref, ch_ref, sw_ref, out_ref, place_ref, row_ref):
    o, v = occ_at(), vir_at()
    place(aux_ref, place_ref)
    group = iota((1, 128), 1) // 16
    y_row = jnp.broadcast_to(vir_ref[...], (8, 128))
    mine = jnp.zeros((8 * SL, 128), F32)
    label = jnp.zeros((8, 128), jnp.int32)
    for x in range(8):
        shift = lax.rem(16 * x + 128 - 16 * o, 128)
        block = jnp.concatenate([r1_ref[p, x * SL : (x + 1) * SL, :] for p in range(8)], axis=0)
        mine = jnp.where(group == x, pltpu.roll(block, shift, 1), mine)
        label = jnp.where(group == x, pltpu.roll(y_row, shift, 1) ^ vir_s[v * 8 + x], label)
    mine = jnp.transpose(jnp.concatenate([mine, jnp.zeros((256 - 8 * SL, 128), F32)], axis=0))
    label = jnp.transpose(jnp.broadcast_to(label[0:1], (128, 128)))
    label = jnp.concatenate([label, label], axis=1)
    hi, lo = split(mine)
    hi, lo = hi.astype(F32), lo.astype(F32)
    total = jnp.zeros((256, 128), F32)
    for g in range(NG):
        both = jnp.concatenate([jnp.where(label == g, hi, 0.0), jnp.where(label == g, lo, 0.0)], axis=0)
        total = total + dot(both.astype(BF16), place_ref[g * 256 : (g + 1) * 256, :].astype(BF16))
    row_ref[0] = total[:128] + total[128:]
    row_ref[1] = jnp.transpose(
        jnp.concatenate([r1_ref[p, 8 * SL : 8 * SL + 16, :] for p in range(8)], axis=0)
    )
    for d in range(16):
        own = row_ref[0, pl.ds(d, 8, stride=16), :]
        amps = row_ref[1, pl.ds(d, 8, stride=16), :]
        for peer in range(8):
            out_ref[peer, d * 8 : d * 8 + 8, :] = own
            out_ref[peer, 128 + d * 8 : 136 + d * 8, :] = amps
    for peer in range(8):
        out_ref[peer, 256:288, :] = ch_ref[...]
        out_ref[peer, 288:304, :] = sw_ref[16 * peer : 16 * peer + 16, :]


def refold_rows(vir_s, aux_ref, vir_ref, r1_ref, out_ref, place_ref):
    v = vir_at()
    place(aux_ref, place_ref)
    spread = jnp.concatenate(
        [jnp.transpose(place_ref[128 * n : 128 * n + 128, :]).astype(BF16) for n in range(2 * NG)], axis=1
    )
    y_row = vir_ref[...]
    pad = jnp.zeros((256 - 8 * SL, 128), F32)
    for x in range(8):
        label = y_row ^ vir_s[v * 8 + x]
        block = jnp.concatenate([r1_ref[p, x * SL : (x + 1) * SL, :] for p in range(8)] + [pad], axis=0)
        hi, lo = split(block)
        both = jnp.concatenate([hi, lo], axis=1)
        total = jnp.zeros((SG, 256), F32)
        for g in range(NG):
            keep = (label == g).astype(F32)
            keep = jnp.concatenate([keep, keep], axis=1).astype(BF16)
            total = total + dot(spread[:, g * 256 : (g + 1) * 256], both * keep)
        hi, lo = split(total[:, :128] + total[:, 128:])
        out_ref[0:128, x * 128 : x * 128 + 128] = hi
        out_ref[128:256, x * 128 : x * 128 + 128] = lo
        out_ref[256:384, x * 128 : x * 128 + 128] = hi


def cycle_first(occ_s, vir_ref, r2_ref, o2_ref, t_ref, y_ref, chat_ref, got_ref):
    o, core = occ_at(), lax.axis_index("core")
    for p in range(8):
        got_ref[2 * p + core] = r2_ref[p, 256:304, :]
        got_ref[2 * p + 1 - core] = o2_ref[p, 256:304, :]
    for k in range(4):
        for n in range(16):
            chat_ref[k * 128 + n * 8 : k * 128 + n * 8 + 8, :] = got_ref[n, 8 * k : 8 * k + 8, :]
    group = iota((8, 128), 1) // 8
    blocks = [got_ref[n, pl.ds(pl.multiple_of(32 + 8 * core, 8), 8), :] for n in range(16)]
    u = []
    for i in range(4):
        row = []
        for k in range(4):
            swapped = jnp.zeros((8, 128), F32)
            for n in range(16):
                shift = (8 * (n - 4 * i - k)) % 128
                swapped = jnp.where(group == n, pltpu.roll(blocks[n], shift, 1) if shift else blocks[n], swapped)
            row.append(2.0 * t_ref[i, k] - swapped)
        u.append(jnp.concatenate(row, axis=1))
    u = jnp.concatenate(u, axis=0)
    label = jnp.concatenate([vir_ref[...] ^ occ_s[o * 4 + k] for k in range(4)], axis=1)
    rows = jnp.concatenate([jnp.where(label == g, u, 0.0) for g in range(NG)], axis=0)
    y = jnp.dot(rows, chat_ref[...], precision=HIGHEST, preferred_element_type=F32)
    y_ref[...] = y.reshape(8, 32, 128)


def ladder(vir_s, vir_ref, b1_ref, r2_ref, o2_ref, out_ref, f_ref, t_ref, hi_ref, lo_ref, acc_ref):
    o, v, core = occ_at(), vir_at(), lax.axis_index("core")
    for ref, part in ((r2_ref, core), (o2_ref, 1 - core)):
        for p in range(8):
            f_ref[:, 2 * p + part] = ref[p, 0:128, :].reshape(16, 8, 128)
            t_ref[:, 2 * p + part] = ref[p, 128:256, :].reshape(16, 8, 128)
    acc_ref[...] = jnp.zeros_like(acc_ref)
    c_lane = jnp.broadcast_to(vir_ref[...], (128, 128))
    bc = jnp.transpose(c_lane) ^ c_lane

    def step(n, carry):
        amps = []
        for half in range(2):
            d = 2 * n + half
            hi, lo = split(f_ref[d].reshape(128, 128))
            w = dot(jnp.concatenate([hi, hi, lo], axis=1), b1_ref[...])
            d_label = vir_s[o * 16 + d]
            for a in range(8):
                keep = bc == (vir_s[v * 8 + a] ^ d_label)
                hi, lo = split(jnp.where(keep, w[:, a * 128 : a * 128 + 128], 0.0))
                hi_ref[a * 128 : a * 128 + 128, half * 128 : half * 128 + 128] = hi
                lo_ref[a * 128 : a * 128 + 128, half * 128 : half * 128 + 128] = lo
            amps.append(t_ref[d].reshape(128, 128))
        hi, lo = split(jnp.concatenate(amps, axis=0))
        r = dot(hi_ref[...], jnp.concatenate([hi, lo], axis=1))
        acc_ref[...] += r[:, :128] + r[:, 128:] + dot(lo_ref[...], hi)
        return carry

    lax.fori_loop(0, 8, step, 0)
    for a in range(8):
        rows = jnp.transpose(acc_ref[a * 128 : a * 128 + 128, :])
        for p in range(8):
            out_ref[p, a] = rows[16 * p : 16 * p + 16, :]


def join(p3_ref, y_ref, out_ref):
    y = y_ref[0]
    for p in range(1, 8):
        y = y + y_ref[p]
    for p in range(8):
        out_ref[p, 0:128, :] = p3_ref[p].reshape(128, 128)
        out_ref[p, 128:160, :] = y


def finish(occ_s, vir_ref, r3_ref, chat_ref, out_ref, sum_ref):
    o = occ_at()
    total = r3_ref[0, 0:128, :]
    for p in range(1, 8):
        total = total + r3_ref[p, 0:128, :]
    sum_ref[...] = total
    z = dot_t(jnp.concatenate([r3_ref[p, 128:160, :] for p in range(8)], axis=0), chat_ref[...], HIGHEST)
    for j in range(4):
        label = vir_ref[...] ^ occ_s[o * 4 + j]
        part = jnp.zeros((32, 128), F32)
        for g in range(NG):
            part = jnp.where(label == g, z[g * 32 : g * 32 + 32, j * 128 : j * 128 + 128], part)
        for i in range(4):
            out_ref[i, j] = sum_ref[pl.ds(i * 4 + j, 8, stride=16), :] + part[8 * i : 8 * i + 8, :]


def swap(x, axes):
    return lax.all_to_all(x, axes, 0, 0, tiled=True)


def folded(t, b, c, occ, vir, aux):
    aux, row = aux.reshape(6, 128), vir.reshape(1, 128)
    shape = jax.ShapeDtypeStruct
    p1 = call(
        fold_local, shape((8, 8 * SL + 16, 128), F32), 1, 4, [pltpu.VMEM((8, 16, 8, 128), F32)],
        (2 * 2 * 24 * 96 * 1024, 1300000),
    )(vir, aux, row, b, t)
    r1 = swap(p1, OCC)
    ch, sw, fits = pl.pallas_call(
        fold_ov,
        out_shape=(shape((32, 128), F32), shape((128, 128), F32), shape((1,), jnp.int32)),
        in_specs=[SMEM, SMEM, VMEM, VMEM, VMEM],
        out_specs=(VMEM, VMEM, SMEM),
        compiler_params=pltpu.CompilerParams(vmem_limit_bytes=LIMIT),
        cost_estimate=pl.CostEstimate(flops=2 * 8 * 768 * 768, bytes_accessed=300000, transcendentals=0),
    )(vir, occ, aux, jnp.transpose(c, (1, 2, 0)), t)
    p2 = call(
        refold_own, shape((8, 304, 128), F32), 1, 5, [pltpu.VMEM((2048, 128), F32), pltpu.VMEM((2, 128, 128), F32)],
        (2 * 256 * 2048 * 128, 2300000),
    )(vir, aux, row, r1, ch, sw)
    r2 = swap(p2, ZY)
    b1 = call(
        refold_rows, shape((384, 1024), BF16), 1, 3, [pltpu.VMEM((2048, 128), F32)], (2 * 128 * 2048 * 2048, 1700000)
    )(vir, aux, row, r1)
    o2 = lax.ppermute(r2, "core", [(0, 1), (1, 0)])
    yp, chat = call(
        cycle_first, (shape((8, 32, 128), F32), shape((512, 128), F32)), 1, 4, [pltpu.VMEM((16, 48, 128), F32)],
        (6 * 2 * 256 * 512 * 128, 4000000),
    )(occ, row, r2, o2, t)
    yr = swap(yp, OCC)
    p3 = call(
        ladder, shape((8, 8, 16, 128), F32), 1, 4,
        [
            pltpu.VMEM((16, 16, 8, 128), F32),
            pltpu.VMEM((16, 16, 8, 128), F32),
            pltpu.VMEM((1024, 256), BF16),
            pltpu.VMEM((1024, 256), BF16),
            pltpu.VMEM((1024, 128), F32),
        ],
        (6 * 2048 * 1024 * 256, 4000000),
    )(vir, row, b1, r2, o2)
    r3 = swap(call(join, shape((8, 160, 128), F32), 0, 2, (), (0, 1300000))(p3, yr), OCC)
    out = call(
        finish, shape((4, 4, 8, 128), F32), 1, 3, [pltpu.VMEM((128, 128), F32)], (6 * 2 * 256 * 512 * 128, 2000000)
    )(occ, row, r3, chat)
    return out, fits


def allowed(left, right, target):
    return (jnp.bitwise_xor(left, right) == target).astype(F32)


def dense(t, b, c, occ, vir, aux):
    o, v = occ_at(), vir_at()
    aux_mine = lax.dynamic_slice_in_dim(aux, o * 96, 96)
    vir_mine = lax.dynamic_slice_in_dim(vir, v * 8, 8)
    occ_mine = lax.dynamic_slice_in_dim(occ, o * 4, 4)
    own = b * allowed(vir_mine[None, :, None], vir[None, None, :], aux_mine[:, None, None])
    wide = lax.all_gather(b, VIR, axis=1, tiled=True)
    wide = wide * allowed(vir[None, :, None], vir[None, None, :], aux_mine[:, None, None])
    pairs = lax.all_gather(t, OCC, axis=1, tiled=True)
    inter = jnp.einsum("qac,qbd->acbd", own, wide, precision=HIGHEST)
    part = jnp.einsum("ijcd,acbd->ijab", lax.all_gather(pairs, VIR, axis=2, tiled=True), inter, precision=HIGHEST)
    total = lax.psum_scatter(part, OCC, scatter_dimension=1, tiled=True)
    swapped = lax.all_to_all(t, VIR, split_axis=3, concat_axis=2, tiled=True)
    u = 2.0 * t - jnp.transpose(swapped, (0, 1, 3, 2))
    cw = lax.all_gather(c, VIR, axis=2, tiled=True)
    cw = cw * allowed(occ_mine[None, :, None], vir[None, None, :], aux[:, None, None])
    y = lax.psum(jnp.einsum("ikac,qkc->iaq", u, cw, precision=HIGHEST), OCC)
    return total + jnp.einsum("iaq,qjb->ijab", y, cw, precision=HIGHEST)


def shards(t, b, c, occ, vir, aux):
    fast, fits = folded(t, b, c, occ, vir, aux)
    return lax.cond(fits[0] > 0, lambda *_: fast, dense, t, b, c, occ, vir, aux)


def solution(mesh):
    fine = Mesh(mesh.devices.reshape(2, 4, 4, 2, 2), ("yh", "x", "z", "yl", "core"))
    placed = (P(None, OCC, VIR, None), P(OCC, VIR, None), P(None, OCC, VIR), P(), P(), P())
    return jax.shard_map(shards, mesh=fine, in_specs=placed, out_specs=P(None, OCC, VIR, None), check_vma=False)
```

```python
import functools

import jax
import jax.numpy as jnp
from jax import lax
from jax.experimental import pallas as pl
from jax.experimental.pallas import tpu as pltpu
from jax.sharding import Mesh, PartitionSpec as P

OCC = ("yh", "x")
ZY = ("z", "yl")
VIR = ("z", "yl", "core")
F32 = jnp.float32
BF16 = jnp.bfloat16
HIGHEST = lax.Precision.HIGHEST
SL = 24
SG = 128
NG = 8
VMEM = pl.BlockSpec(memory_space=pltpu.VMEM)
SMEM = pl.BlockSpec(memory_space=pltpu.SMEM)
LIMIT = 14 * 2**20


def occ_at():
    return lax.axis_index("yh") * 4 + lax.axis_index("x")


def vir_at():
    return lax.axis_index("z") * 4 + lax.axis_index("yl") * 2 + lax.axis_index("core")


def iota(shape, dim):
    return lax.broadcasted_iota(jnp.int32, shape, dim)


def split(x):
    hi = x.astype(BF16)
    return hi, (x - hi.astype(F32)).astype(BF16)


def dot(x, y):
    return jnp.dot(x, y, preferred_element_type=F32)


def dot_t(x, y, precision=None):
    return lax.dot_general(x, y, (((1,), (1,)), ((), ())), precision=precision, preferred_element_type=F32)


def call(body, outs, n_smem, n_vmem, scratch=(), cost=(0, 0), limit=LIMIT):
    return pl.pallas_call(
        body,
        out_shape=outs,
        in_specs=[SMEM] * n_smem + [VMEM] * n_vmem,
        out_specs=jax.tree.map(lambda _: VMEM, outs),
        scratch_shapes=list(scratch),
        compiler_params=pltpu.CompilerParams(vmem_limit_bytes=limit),
        cost_estimate=pl.CostEstimate(flops=cost[0], bytes_accessed=cost[1], transcendentals=0),
    )


def aux_block(aux_ref, block):
    row, skip = lax.div(3 * block, 4), 32 * lax.rem(3 * block, 4)
    first = jnp.broadcast_to(aux_ref[pl.ds(row, 1), :], (8, 128))
    second = jnp.broadcast_to(aux_ref[pl.ds(jnp.minimum(row + 1, 5), 1), :], (8, 128))
    lane = iota((8, 128), 1)
    shift = lax.rem(128 - skip, 128)
    joined = jnp.where(lane < 128 - skip, pltpu.roll(first, shift, 1), pltpu.roll(second, shift, 1))
    return jnp.where(lane < 96, joined, NG)


def aux_blocks(aux_ref):
    rows = jnp.zeros((8, 128), jnp.int32)
    for block in range(8):
        rows = jnp.where(iota((8, 128), 0) == block, aux_block(aux_ref, jnp.int32(block)), rows)
    return rows


def fold_local(vir_s, aux_ref, vir_ref, b_ref, t_ref, out_ref, roll_ref):
    o, v = occ_at(), vir_at()
    q_lane = jnp.broadcast_to(aux_block(aux_ref, o)[0:1], (128, 128))
    q_sub = jnp.transpose(q_lane)
    same = (q_sub == q_lane) & (iota((128, 128), 0) < iota((128, 128), 1))
    rank = jnp.sum(same.astype(F32), axis=0, keepdims=True)
    pick = (rank == iota((SL, 128), 0).astype(F32)).astype(F32)[:, :96].astype(BF16)
    y_row = vir_ref[...]
    for x in range(8):
        keep = (y_row ^ vir_s[v * 8 + x]) == q_sub[:96]
        hi, lo = split(jnp.where(keep, b_ref[:, x, :], 0.0))
        folded = dot(pick, hi) + dot(pick, lo)
        for peer in range(8):
            out_ref[peer, x * SL : (x + 1) * SL, :] = folded
    amps = t_ref[...].reshape(16, 8, 128)
    for k in range(8):
        roll_ref[k] = pltpu.roll(amps, 16 * k, 2) if k else amps
    group = iota((16, 128), 1) // 16
    for peer in range(8):
        block = jnp.zeros((16, 128), F32)
        for c in range(8):
            block = jnp.where(group == c, roll_ref[(c - peer) % 8, :, c, :], block)
        out_ref[peer, 8 * SL : 8 * SL + 16, :] = block


def fold_ov(vir_s, occ_s, aux_ref, c_ref, t_ref, ch_ref, sw_ref, fits_ref):
    o, v = occ_at(), vir_at()
    rows = aux_blocks(aux_ref)
    over = jnp.zeros((8, 1), F32)
    for g in range(NG):
        count = jnp.sum((rows == g).astype(F32), axis=1, keepdims=True)
        over = jnp.maximum(over, jnp.maximum(count - SL, jnp.sum(count, axis=0, keepdims=True) - SG))
    fits_ref[0] = (jnp.max(over) < 0.5).astype(jnp.int32)
    aux = jnp.concatenate([aux_ref[n : n + 1, :] for n in range(6)], axis=1)
    member = (aux == iota((NG, 768), 0)).astype(F32)
    before = (iota((768, 768), 0) < iota((768, 768), 1)).astype(F32).astype(BF16)
    rank = jnp.sum(member * dot(member.astype(BF16), before), axis=0, keepdims=True)
    pick = (rank == iota((SG, 768), 0).astype(F32)).astype(F32).astype(BF16)
    c_label = jnp.zeros((8, 1), jnp.int32)
    for c in range(8):
        c_label = jnp.where(iota((8, 1), 0) == c, vir_s[v * 8 + c], c_label)
    for k in range(4):
        keep = (c_label ^ occ_s[o * 4 + k]) == aux
        hi, lo = split(jnp.where(keep, c_ref[k], 0.0))
        ch_ref[8 * k : 8 * k + 8, :] = dot_t(hi, pick) + dot_t(lo, pick)
    sw_ref[...] = jnp.transpose(t_ref[...].reshape(128, 128))


def place(aux_ref, place_ref):
    lane = iota((SL, 128), 1).astype(F32) - iota((SL, 128), 0).astype(F32)
    aux = aux_blocks(aux_ref)
    for g in range(NG):
        count = jnp.sum((aux == g).astype(F32), axis=1, keepdims=True)
        start = jnp.zeros((1, 1), F32)
        for block in range(8):
            row = g * 256 + block * SL
            place_ref[row : row + SL, :] = (lane == start).astype(F32)
            start = start + count[block : block + 1, :]
        place_ref[g * 256 + 8 * SL : (g + 1) * 256, :] = jnp.zeros((256 - 8 * SL, 128), F32)


def refold_own(vir_s, aux_ref, vir_ref, r1_ref, ch_ref, sw_ref, out_ref, place_ref, row_ref):
    o, v = occ_at(), vir_at()
    place(aux_ref, place_ref)
    group = iota((1, 128), 1) // 16
    y_row = jnp.broadcast_to(vir_ref[...], (8, 128))
    mine = jnp.zeros((8 * SL, 128), F32)
    label = jnp.zeros((8, 128), jnp.int32)
    for x in range(8):
        shift = lax.rem(16 * x + 128 - 16 * o, 128)
        block = jnp.concatenate([r1_ref[p, x * SL : (x + 1) * SL, :] for p in range(8)], axis=0)
        mine = jnp.where(group == x, pltpu.roll(block, shift, 1), mine)
        label = jnp.where(group == x, pltpu.roll(y_row, shift, 1) ^ vir_s[v * 8 + x], label)
    mine = jnp.transpose(jnp.concatenate([mine, jnp.zeros((256 - 8 * SL, 128), F32)], axis=0))
    label = jnp.transpose(jnp.broadcast_to(label[0:1], (128, 128)))
    label = jnp.concatenate([label, label], axis=1)
    hi, lo = split(mine)
    hi, lo = hi.astype(F32), lo.astype(F32)
    total = jnp.zeros((256, 128), F32)
    for g in range(NG):
        both = jnp.concatenate([jnp.where(label == g, hi, 0.0), jnp.where(label == g, lo, 0.0)], axis=0)
        total = total + dot(both.astype(BF16), place_ref[g * 256 : (g + 1) * 256, :].astype(BF16))
    row_ref[0] = total[:128] + total[128:]
    row_ref[1] = jnp.transpose(
        jnp.concatenate([r1_ref[p, 8 * SL : 8 * SL + 16, :] for p in range(8)], axis=0)
    )
    for d in range(16):
        own = row_ref[0, pl.ds(d, 8, stride=16), :]
        amps = row_ref[1, pl.ds(d, 8, stride=16), :]
        for peer in range(8):
            out_ref[peer, d * 8 : d * 8 + 8, :] = own
            out_ref[peer, 128 + d * 8 : 136 + d * 8, :] = amps
    for peer in range(8):
        out_ref[peer, 256:288, :] = ch_ref[...]
        out_ref[peer, 288:304, :] = sw_ref[16 * peer : 16 * peer + 16, :]


def refold_rows(vir_s, aux_ref, vir_ref, r1_ref, out_ref, place_ref):
    v = vir_at()
    place(aux_ref, place_ref)
    spread = jnp.concatenate(
        [jnp.transpose(place_ref[128 * n : 128 * n + 128, :]).astype(BF16) for n in range(2 * NG)], axis=1
    )
    y_row = vir_ref[...]
    pad = jnp.zeros((256 - 8 * SL, 128), F32)
    for x in range(8):
        label = y_row ^ vir_s[v * 8 + x]
        block = jnp.concatenate([r1_ref[p, x * SL : (x + 1) * SL, :] for p in range(8)] + [pad], axis=0)
        hi, lo = split(block)
        both = jnp.concatenate([hi, lo], axis=1)
        total = jnp.zeros((SG, 256), F32)
        for g in range(NG):
            keep = (label == g).astype(F32)
            keep = jnp.concatenate([keep, keep], axis=1).astype(BF16)
            total = total + dot(spread[:, g * 256 : (g + 1) * 256], both * keep)
        hi, lo = split(total[:, :128] + total[:, 128:])
        out_ref[0:128, x * 128 : x * 128 + 128] = hi
        out_ref[128:256, x * 128 : x * 128 + 128] = lo
        out_ref[256:384, x * 128 : x * 128 + 128] = hi


def cycle_first(occ_s, vir_ref, r2_ref, o2_ref, t_ref, y_ref, chat_ref, got_ref):
    o, core = occ_at(), lax.axis_index("core")
    for p in range(8):
        got_ref[2 * p + core] = r2_ref[p, 256:304, :]
        got_ref[2 * p + 1 - core] = o2_ref[p, 256:304, :]
    for k in range(4):
        for n in range(16):
            chat_ref[k * 128 + n * 8 : k * 128 + n * 8 + 8, :] = got_ref[n, 8 * k : 8 * k + 8, :]
    group = iota((8, 128), 1) // 8
    blocks = [got_ref[n, pl.ds(pl.multiple_of(32 + 8 * core, 8), 8), :] for n in range(16)]
    u = []
    for i in range(4):
        row = []
        for k in range(4):
            swapped = jnp.zeros((8, 128), F32)
            for n in range(16):
                shift = (8 * (n - 4 * i - k)) % 128
                swapped = jnp.where(group == n, pltpu.roll(blocks[n], shift, 1) if shift else blocks[n], swapped)
            row.append(2.0 * t_ref[i, k] - swapped)
        u.append(jnp.concatenate(row, axis=1))
    u = jnp.concatenate(u, axis=0)
    label = jnp.concatenate([vir_ref[...] ^ occ_s[o * 4 + k] for k in range(4)], axis=1)
    rows = jnp.concatenate([jnp.where(label == g, u, 0.0) for g in range(NG)], axis=0)
    y = jnp.dot(rows, chat_ref[...], precision=HIGHEST, preferred_element_type=F32)
    y_ref[...] = y.reshape(8, 32, 128)


def ladder(vir_s, vir_ref, b1_ref, r2_ref, o2_ref, out_ref, f_ref, t_ref, hi_ref, lo_ref, acc_ref):
    o, v, core = occ_at(), vir_at(), lax.axis_index("core")
    for ref, part in ((r2_ref, core), (o2_ref, 1 - core)):
        for p in range(8):
            f_ref[:, 2 * p + part] = ref[p, 0:128, :].reshape(16, 8, 128)
            t_ref[:, 2 * p + part] = ref[p, 128:256, :].reshape(16, 8, 128)
    acc_ref[...] = jnp.zeros_like(acc_ref)
    c_lane = jnp.broadcast_to(vir_ref[...], (128, 128))
    bc = jnp.transpose(c_lane) ^ c_lane

    def step(n, carry):
        amps = []
        for half in range(2):
            d = 2 * n + half
            hi, lo = split(f_ref[d].reshape(128, 128))
            w = dot(jnp.concatenate([hi, hi, lo], axis=1), b1_ref[...])
            d_label = vir_s[o * 16 + d]
            for a in range(8):
                keep = bc == (vir_s[v * 8 + a] ^ d_label)
                hi, lo = split(jnp.where(keep, w[:, a * 128 : a * 128 + 128], 0.0))
                hi_ref[a * 128 : a * 128 + 128, half * 128 : half * 128 + 128] = hi
                lo_ref[a * 128 : a * 128 + 128, half * 128 : half * 128 + 128] = lo
            amps.append(t_ref[d].reshape(128, 128))
        hi, lo = split(jnp.concatenate(amps, axis=0))
        r = dot(hi_ref[...], jnp.concatenate([hi, lo], axis=1))
        acc_ref[...] += r[:, :128] + r[:, 128:] + dot(lo_ref[...], hi)
        return carry

    lax.fori_loop(0, 8, step, 0, unroll=True)
    for a in range(8):
        rows = jnp.transpose(acc_ref[a * 128 : a * 128 + 128, :])
        for p in range(8):
            out_ref[p, a] = rows[16 * p : 16 * p + 16, :]


def join(p3_ref, y_ref, out_ref):
    y = y_ref[0]
    for p in range(1, 8):
        y = y + y_ref[p]
    for p in range(8):
        out_ref[p, 0:128, :] = p3_ref[p].reshape(128, 128)
        out_ref[p, 128:160, :] = y


def finish(occ_s, vir_ref, r3_ref, chat_ref, out_ref, sum_ref):
    o = occ_at()
    total = r3_ref[0, 0:128, :]
    for p in range(1, 8):
        total = total + r3_ref[p, 0:128, :]
    sum_ref[...] = total
    z = dot_t(jnp.concatenate([r3_ref[p, 128:160, :] for p in range(8)], axis=0), chat_ref[...], HIGHEST)
    for j in range(4):
        label = vir_ref[...] ^ occ_s[o * 4 + j]
        part = jnp.zeros((32, 128), F32)
        for g in range(NG):
            part = jnp.where(label == g, z[g * 32 : g * 32 + 32, j * 128 : j * 128 + 128], part)
        for i in range(4):
            out_ref[i, j] = sum_ref[pl.ds(i * 4 + j, 8, stride=16), :] + part[8 * i : 8 * i + 8, :]


def swap(x, axes):
    return lax.all_to_all(x, axes, 0, 0, tiled=True)


def folded(t, b, c, occ, vir, aux):
    aux, row = aux.reshape(6, 128), vir.reshape(1, 128)
    shape = jax.ShapeDtypeStruct
    p1 = call(
        fold_local, shape((8, 8 * SL + 16, 128), F32), 1, 4, [pltpu.VMEM((8, 16, 8, 128), F32)],
        (2 * 2 * 24 * 96 * 1024, 1300000), 56 * 2**20,
    )(vir, aux, row, b, t)
    r1 = swap(p1, OCC)
    ch, sw, fits = pl.pallas_call(
        fold_ov,
        out_shape=(shape((32, 128), F32), shape((128, 128), F32), shape((1,), jnp.int32)),
        in_specs=[SMEM, SMEM, VMEM, VMEM, VMEM],
        out_specs=(VMEM, VMEM, SMEM),
        compiler_params=pltpu.CompilerParams(vmem_limit_bytes=LIMIT),
        cost_estimate=pl.CostEstimate(flops=2 * 8 * 768 * 768, bytes_accessed=300000, transcendentals=0),
    )(vir, occ, aux, jnp.transpose(c, (1, 2, 0)), t)
    p2 = call(
        refold_own, shape((8, 304, 128), F32), 1, 5, [pltpu.VMEM((2048, 128), F32), pltpu.VMEM((2, 128, 128), F32)],
        (2 * 256 * 2048 * 128, 2300000),
    )(vir, aux, row, r1, ch, sw)
    r2 = swap(p2, ZY)
    b1 = call(
        refold_rows, shape((384, 1024), BF16), 1, 3, [pltpu.VMEM((2048, 128), F32)], (2 * 128 * 2048 * 2048, 1700000)
    )(vir, aux, row, r1)
    o2 = lax.ppermute(r2, "core", [(0, 1), (1, 0)])
    yp, chat = call(
        cycle_first, (shape((8, 32, 128), F32), shape((512, 128), F32)), 1, 4, [pltpu.VMEM((16, 48, 128), F32)],
        (6 * 2 * 256 * 512 * 128, 4000000),
    )(occ, row, r2, o2, t)
    yr = swap(yp, OCC)
    p3 = call(
        ladder, shape((8, 8, 16, 128), F32), 1, 4,
        [
            pltpu.VMEM((16, 16, 8, 128), F32),
            pltpu.VMEM((16, 16, 8, 128), F32),
            pltpu.VMEM((1024, 256), BF16),
            pltpu.VMEM((1024, 256), BF16),
            pltpu.VMEM((1024, 128), F32),
        ],
        (6 * 2048 * 1024 * 256, 4000000),
    )(vir, row, b1, r2, o2)
    r3 = swap(call(join, shape((8, 160, 128), F32), 0, 2, (), (0, 1300000))(p3, yr), OCC)
    out = call(
        finish, shape((4, 4, 8, 128), F32), 1, 3, [pltpu.VMEM((128, 128), F32)], (6 * 2 * 256 * 512 * 128, 2000000)
    )(occ, row, r3, chat)
    return out, fits


def allowed(left, right, target):
    return (jnp.bitwise_xor(left, right) == target).astype(F32)


def gather(x, axes, n, dim):
    parts = swap(jnp.broadcast_to(x[None], (n,) + x.shape), axes)
    return jnp.concatenate([parts[p] for p in range(n)], axis=dim)


def dense(t, b, c, occ, vir, aux):
    o, v = occ_at(), vir_at()
    aux_mine = lax.dynamic_slice_in_dim(aux, o * 96, 96)
    vir_mine = lax.dynamic_slice_in_dim(vir, v * 8, 8)
    occ_mine = lax.dynamic_slice_in_dim(occ, o * 4, 4)
    own = b * allowed(vir_mine[None, :, None], vir[None, None, :], aux_mine[:, None, None])
    wide = gather(b, VIR, 16, 1)
    wide = wide * allowed(vir[None, :, None], vir[None, None, :], aux_mine[:, None, None])
    pairs = gather(t, OCC, 8, 1)
    inter = jnp.einsum("qac,qbd->acbd", own, wide, precision=HIGHEST)
    part = jnp.einsum("ijcd,acbd->ijab", gather(pairs, VIR, 16, 2), inter, precision=HIGHEST)
    total = jnp.sum(swap(jnp.moveaxis(part.reshape(4, 8, 4, 8, 128), 1, 0), OCC), axis=0)
    swapped = lax.all_to_all(t, VIR, split_axis=3, concat_axis=2, tiled=True)
    u = 2.0 * t - jnp.transpose(swapped, (0, 1, 3, 2))
    cw = gather(c, VIR, 16, 2)
    cw = cw * allowed(occ_mine[None, :, None], vir[None, None, :], aux[:, None, None])
    part = jnp.einsum("ikac,qkc->iaq", u, cw, precision=HIGHEST)
    y = jnp.sum(swap(jnp.broadcast_to(part[None], (8,) + part.shape), OCC), axis=0)
    return total + jnp.einsum("iaq,qjb->ijab", y, cw, precision=HIGHEST)


def shards(t, b, c, occ, vir, aux):
    fast, fits = folded(t, b, c, occ, vir, aux)
    return lax.cond(fits[0] > 0, lambda *_: fast, dense, t, b, c, occ, vir, aux)


def solution(mesh):
    fine = Mesh(mesh.devices.reshape(2, 4, 4, 2, 2), ("yh", "x", "z", "yl", "core"))
    placed = (P(None, OCC, VIR, None), P(OCC, VIR, None), P(None, OCC, VIR), P(), P(), P())
    return jax.shard_map(shards, mesh=fine, in_specs=placed, out_specs=P(None, OCC, VIR, None), check_vma=False)
```

```python
import functools

import jax
import jax.numpy as jnp
from jax import lax
from jax.experimental import pallas as pl
from jax.experimental.pallas import tpu as pltpu
from jax.sharding import Mesh, PartitionSpec as P

OCC = ("yh", "x")
ZY = ("z", "yl")
VIR = ("z", "yl", "core")
F32 = jnp.float32
BF16 = jnp.bfloat16
HIGHEST = lax.Precision.HIGHEST
SL = 24
SG = 128
NG = 8
VMEM = pl.BlockSpec(memory_space=pltpu.VMEM)
SMEM = pl.BlockSpec(memory_space=pltpu.SMEM)
LIMIT = 14 * 2**20


def occ_at():
    return lax.axis_index("yh") * 4 + lax.axis_index("x")


def vir_at():
    return lax.axis_index("z") * 4 + lax.axis_index("yl") * 2 + lax.axis_index("core")


def iota(shape, dim):
    return lax.broadcasted_iota(jnp.int32, shape, dim)


def split(x):
    hi = x.astype(BF16)
    return hi, (x - hi.astype(F32)).astype(BF16)


def dot(x, y):
    return jnp.dot(x, y, preferred_element_type=F32)


def dot_t(x, y, precision=None):
    return lax.dot_general(x, y, (((1,), (1,)), ((), ())), precision=precision, preferred_element_type=F32)


def call(body, outs, n_smem, n_vmem, scratch=(), cost=(0, 0), limit=LIMIT):
    return pl.pallas_call(
        body,
        out_shape=outs,
        in_specs=[SMEM] * n_smem + [VMEM] * n_vmem,
        out_specs=jax.tree.map(lambda _: VMEM, outs),
        scratch_shapes=list(scratch),
        compiler_params=pltpu.CompilerParams(vmem_limit_bytes=limit),
        cost_estimate=pl.CostEstimate(flops=cost[0], bytes_accessed=cost[1], transcendentals=0),
    )


def aux_block(aux_ref, block):
    row, skip = lax.div(3 * block, 4), 32 * lax.rem(3 * block, 4)
    first = jnp.broadcast_to(aux_ref[pl.ds(row, 1), :], (8, 128))
    second = jnp.broadcast_to(aux_ref[pl.ds(jnp.minimum(row + 1, 5), 1), :], (8, 128))
    lane = iota((8, 128), 1)
    shift = lax.rem(128 - skip, 128)
    joined = jnp.where(lane < 128 - skip, pltpu.roll(first, shift, 1), pltpu.roll(second, shift, 1))
    return jnp.where(lane < 96, joined, NG)


def aux_blocks(aux_ref):
    rows = jnp.zeros((8, 128), jnp.int32)
    for block in range(8):
        rows = jnp.where(iota((8, 128), 0) == block, aux_block(aux_ref, jnp.int32(block)), rows)
    return rows


def fold_local(vir_s, aux_ref, vir_ref, b_ref, t_ref, out_ref, roll_ref):
    o, v = occ_at(), vir_at()
    q_lane = jnp.broadcast_to(aux_block(aux_ref, o)[0:1], (128, 128))
    q_sub = jnp.transpose(q_lane)
    same = (q_sub == q_lane) & (iota((128, 128), 0) < iota((128, 128), 1))
    rank = jnp.sum(same.astype(F32), axis=0, keepdims=True)
    pick = (rank == iota((SL, 128), 0).astype(F32)).astype(F32)[:, :96].astype(BF16)
    y_row = vir_ref[...]
    for x in range(8):
        keep = (y_row ^ vir_s[v * 8 + x]) == q_sub[:96]
        hi, lo = split(jnp.where(keep, b_ref[:, x, :], 0.0))
        folded = dot(pick, hi) + dot(pick, lo)
        for peer in range(8):
            out_ref[peer, x * SL : (x + 1) * SL, :] = folded
    amps = t_ref[...].reshape(16, 8, 128)
    for k in range(8):
        roll_ref[k] = pltpu.roll(amps, 16 * k, 2) if k else amps
    group = iota((16, 128), 1) // 16
    for peer in range(8):
        block = jnp.zeros((16, 128), F32)
        for c in range(8):
            block = jnp.where(group == c, roll_ref[(c - peer) % 8, :, c, :], block)
        out_ref[peer, 8 * SL : 8 * SL + 16, :] = block


def fold_ov(vir_s, occ_s, aux_ref, c_ref, t_ref, ch_ref, sw_ref, fits_ref):
    o, v = occ_at(), vir_at()
    rows = aux_blocks(aux_ref)
    over = jnp.zeros((8, 1), F32)
    for g in range(NG):
        count = jnp.sum((rows == g).astype(F32), axis=1, keepdims=True)
        over = jnp.maximum(over, jnp.maximum(count - SL, jnp.sum(count, axis=0, keepdims=True) - SG))
    fits_ref[0] = (jnp.max(over) < 0.5).astype(jnp.int32)
    aux = jnp.concatenate([aux_ref[n : n + 1, :] for n in range(6)], axis=1)
    member = (aux == iota((NG, 768), 0)).astype(F32)
    before = (iota((768, 768), 0) < iota((768, 768), 1)).astype(F32).astype(BF16)
    rank = jnp.sum(member * dot(member.astype(BF16), before), axis=0, keepdims=True)
    pick = (rank == iota((SG, 768), 0).astype(F32)).astype(F32).astype(BF16)
    c_label = jnp.zeros((8, 1), jnp.int32)
    for c in range(8):
        c_label = jnp.where(iota((8, 1), 0) == c, vir_s[v * 8 + c], c_label)
    for k in range(4):
        keep = (c_label ^ occ_s[o * 4 + k]) == aux
        hi, lo = split(jnp.where(keep, c_ref[k], 0.0))
        ch_ref[8 * k : 8 * k + 8, :] = dot_t(hi, pick) + dot_t(lo, pick)
    sw_ref[...] = jnp.transpose(t_ref[...].reshape(128, 128))


def place(aux_ref, place_ref):
    lane = iota((SL, 128), 1).astype(F32) - iota((SL, 128), 0).astype(F32)
    aux = aux_blocks(aux_ref)
    for g in range(NG):
        count = jnp.sum((aux == g).astype(F32), axis=1, keepdims=True)
        start = jnp.zeros((1, 1), F32)
        for block in range(8):
            row = g * 256 + block * SL
            place_ref[row : row + SL, :] = (lane == start).astype(F32)
            start = start + count[block : block + 1, :]
        place_ref[g * 256 + 8 * SL : (g + 1) * 256, :] = jnp.zeros((256 - 8 * SL, 128), F32)


def refold_own(vir_s, aux_ref, vir_ref, r1_ref, ch_ref, sw_ref, out_ref, place_ref, row_ref):
    o, v = occ_at(), vir_at()
    place(aux_ref, place_ref)
    group = iota((1, 128), 1) // 16
    y_row = jnp.broadcast_to(vir_ref[...], (8, 128))
    mine = jnp.zeros((8 * SL, 128), F32)
    label = jnp.zeros((8, 128), jnp.int32)
    for x in range(8):
        shift = lax.rem(16 * x + 128 - 16 * o, 128)
        block = jnp.concatenate([r1_ref[p, x * SL : (x + 1) * SL, :] for p in range(8)], axis=0)
        mine = jnp.where(group == x, pltpu.roll(block, shift, 1), mine)
        label = jnp.where(group == x, pltpu.roll(y_row, shift, 1) ^ vir_s[v * 8 + x], label)
    mine = jnp.transpose(jnp.concatenate([mine, jnp.zeros((256 - 8 * SL, 128), F32)], axis=0))
    label = jnp.transpose(jnp.broadcast_to(label[0:1], (128, 128)))
    label = jnp.concatenate([label, label], axis=1)
    hi, lo = split(mine)
    hi, lo = hi.astype(F32), lo.astype(F32)
    total = jnp.zeros((256, 128), F32)
    for g in range(NG):
        both = jnp.concatenate([jnp.where(label == g, hi, 0.0), jnp.where(label == g, lo, 0.0)], axis=0)
        total = total + dot(both.astype(BF16), place_ref[g * 256 : (g + 1) * 256, :].astype(BF16))
    row_ref[0] = total[:128] + total[128:]
    row_ref[1] = jnp.transpose(
        jnp.concatenate([r1_ref[p, 8 * SL : 8 * SL + 16, :] for p in range(8)], axis=0)
    )
    for d in range(16):
        own = row_ref[0, pl.ds(d, 8, stride=16), :]
        amps = row_ref[1, pl.ds(d, 8, stride=16), :]
        for peer in range(8):
            out_ref[peer, d * 8 : d * 8 + 8, :] = own
            out_ref[peer, 128 + d * 8 : 136 + d * 8, :] = amps
    for peer in range(8):
        out_ref[peer, 256:288, :] = ch_ref[...]
        out_ref[peer, 288:304, :] = sw_ref[16 * peer : 16 * peer + 16, :]


def refold_rows(vir_s, aux_ref, vir_ref, r1_ref, out_ref, place_ref):
    v = vir_at()
    place(aux_ref, place_ref)
    spread = jnp.concatenate(
        [jnp.transpose(place_ref[128 * n : 128 * n + 128, :]).astype(BF16) for n in range(2 * NG)], axis=1
    )
    y_row = vir_ref[...]
    pad = jnp.zeros((256 - 8 * SL, 128), F32)
    for x in range(8):
        label = y_row ^ vir_s[v * 8 + x]
        block = jnp.concatenate([r1_ref[p, x * SL : (x + 1) * SL, :] for p in range(8)] + [pad], axis=0)
        hi, lo = split(block)
        both = jnp.concatenate([hi, lo], axis=1)
        total = jnp.zeros((SG, 256), F32)
        for g in range(NG):
            keep = (label == g).astype(F32)
            keep = jnp.concatenate([keep, keep], axis=1).astype(BF16)
            total = total + dot(spread[:, g * 256 : (g + 1) * 256], both * keep)
        out_ref[:, x * 128 : x * 128 + 128] = total[:, :128] + total[:, 128:]


def cycle_first(occ_s, vir_ref, r2_ref, o2_ref, t_ref, b1_ref, y_ref, chat_ref, cat_ref, f_ref, amps_ref, got_ref):
    o, core = occ_at(), lax.axis_index("core")
    for ref, part in ((r2_ref, core), (o2_ref, 1 - core)):
        for p in range(8):
            f_ref[:, 2 * p + part] = ref[p, 0:128, :].reshape(16, 8, 128)
            amps_ref[:, 2 * p + part] = ref[p, 128:256, :].reshape(16, 8, 128)
    for p in range(8):
        got_ref[2 * p + core] = r2_ref[p, 256:304, :]
        got_ref[2 * p + 1 - core] = o2_ref[p, 256:304, :]
    for k in range(4):
        for n in range(16):
            chat_ref[k * 128 + n * 8 : k * 128 + n * 8 + 8, :] = got_ref[n, 8 * k : 8 * k + 8, :]
    group = iota((8, 128), 1) // 8
    blocks = [got_ref[n, pl.ds(pl.multiple_of(32 + 8 * core, 8), 8), :] for n in range(16)]
    u = []
    for i in range(4):
        row = []
        for k in range(4):
            swapped = jnp.zeros((8, 128), F32)
            for n in range(16):
                shift = (8 * (n - 4 * i - k)) % 128
                swapped = jnp.where(group == n, pltpu.roll(blocks[n], shift, 1) if shift else blocks[n], swapped)
            row.append(2.0 * t_ref[i, k] - swapped)
        u.append(jnp.concatenate(row, axis=1))
    u = jnp.concatenate(u, axis=0)
    label = jnp.concatenate([vir_ref[...] ^ occ_s[o * 4 + k] for k in range(4)], axis=1)
    rows = jnp.concatenate([jnp.where(label == g, u, 0.0) for g in range(NG)], axis=0)
    y = jnp.dot(rows, chat_ref[...], precision=lax.Precision.HIGH, preferred_element_type=F32)
    y_ref[...] = y.reshape(8, 32, 128)
    hi, lo = split(b1_ref[...])
    cat_ref[0:128], cat_ref[128:256], cat_ref[256:384] = hi, lo, hi


def ladder(vir_s, vir_ref, b1_ref, f_ref, t_ref, _, acc_ref, hi_ref, lo_ref):
    o, v = occ_at(), vir_at()
    acc_ref[...] = jnp.zeros_like(acc_ref)
    c_lane = jnp.broadcast_to(vir_ref[...], (128, 128))
    bc = jnp.transpose(c_lane) ^ c_lane

    def step(n, carry):
        amps = []
        for half in range(2):
            d = 2 * n + half
            hi, lo = split(f_ref[d].reshape(128, 128))
            w = dot(jnp.concatenate([hi, hi, lo], axis=1), b1_ref[...])
            d_label = vir_s[o * 16 + d]
            for a in range(8):
                keep = bc == (vir_s[v * 8 + a] ^ d_label)
                hi, lo = split(jnp.where(keep, w[:, a * 128 : a * 128 + 128], 0.0))
                hi_ref[a * 128 : a * 128 + 128, half * 128 : half * 128 + 128] = hi
                lo_ref[a * 128 : a * 128 + 128, half * 128 : half * 128 + 128] = lo
            amps.append(t_ref[d].reshape(128, 128))
        hi, lo = split(jnp.concatenate(amps, axis=0))
        r = dot(hi_ref[...], jnp.concatenate([hi, lo], axis=1))
        acc_ref[...] += r[:, :128] + r[:, 128:] + dot(lo_ref[...], hi)
        return carry

    lax.fori_loop(0, 8, step, 0, unroll=True)


def join(p3_ref, y_ref, _, out_ref):
    y = y_ref[0]
    for p in range(1, 8):
        y = y + y_ref[p]
    for a in range(8):
        rows = jnp.transpose(p3_ref[a * 128 : a * 128 + 128, :])
        for p in range(8):
            out_ref[p, 16 * a : 16 * a + 16, :] = rows[16 * p : 16 * p + 16, :]
    for p in range(8):
        out_ref[p, 128:160, :] = y


def finish(occ_s, vir_ref, r3_ref, chat_ref, out_ref, sum_ref):
    o = occ_at()
    total = r3_ref[0, 0:128, :]
    for p in range(1, 8):
        total = total + r3_ref[p, 0:128, :]
    sum_ref[...] = total
    z = dot_t(jnp.concatenate([r3_ref[p, 128:160, :] for p in range(8)], axis=0), chat_ref[...], lax.Precision.HIGH)
    for j in range(4):
        label = vir_ref[...] ^ occ_s[o * 4 + j]
        part = jnp.zeros((32, 128), F32)
        for g in range(NG):
            part = jnp.where(label == g, z[g * 32 : g * 32 + 32, j * 128 : j * 128 + 128], part)
        for i in range(4):
            out_ref[i, j] = sum_ref[pl.ds(i * 4 + j, 8, stride=16), :] + part[8 * i : 8 * i + 8, :]


def swap(x, axes):
    return lax.all_to_all(x, axes, 0, 0, tiled=True)


def folded(t, b, c, occ, vir, aux):
    aux, row = aux.reshape(6, 128), vir.reshape(1, 128)
    shape = jax.ShapeDtypeStruct
    p1 = call(
        fold_local, shape((8, 8 * SL + 16, 128), F32), 1, 4, [pltpu.VMEM((8, 16, 8, 128), F32)],
        (2 * 2 * 24 * 96 * 1024, 1300000), 56 * 2**20,
    )(vir, aux, row, b, t)
    r1 = swap(p1, OCC)
    ch, sw, fits = pl.pallas_call(
        fold_ov,
        out_shape=(shape((32, 128), F32), shape((128, 128), F32), shape((1,), jnp.int32)),
        in_specs=[SMEM, SMEM, VMEM, VMEM, VMEM],
        out_specs=(VMEM, VMEM, SMEM),
        compiler_params=pltpu.CompilerParams(vmem_limit_bytes=LIMIT),
        cost_estimate=pl.CostEstimate(flops=2 * 8 * 768 * 768, bytes_accessed=300000, transcendentals=0),
    )(vir, occ, aux, jnp.transpose(c, (1, 2, 0)), t)
    p2 = call(
        refold_own, shape((8, 304, 128), F32), 1, 5, [pltpu.VMEM((2048, 128), F32), pltpu.VMEM((2, 128, 128), F32)],
        (2 * 256 * 2048 * 128, 2300000),
    )(vir, aux, row, r1, ch, sw)
    r2 = swap(p2, ZY)
    b1 = call(
        refold_rows, shape((SG, 1024), F32), 1, 3, [pltpu.VMEM((2048, 128), F32)], (2 * 128 * 2048 * 2048, 1700000)
    )(vir, aux, row, r1)
    o2 = lax.ppermute(r2, "core", [(0, 1), (1, 0)])
    staged = shape((16, 16, 8, 128), F32)
    yp, chat, cat, f, amps = call(
        cycle_first, (shape((8, 32, 128), F32), shape((512, 128), F32), shape((384, 1024), BF16), staged, staged), 1, 5,
        [pltpu.VMEM((16, 48, 128), F32)],
        (6 * 2 * 256 * 512 * 128, 4000000),
    )(occ, row, r2, o2, t, b1)
    yr = swap(yp, OCC)
    p3 = call(
        ladder, shape((1024, 128), F32), 1, 5,
        [
            pltpu.VMEM((1024, 256), BF16),
            pltpu.VMEM((1024, 256), BF16),
        ],
        (6 * 2048 * 1024 * 256, 4000000),
    )(vir, row, cat, f, amps, chat)
    r3 = swap(call(join, shape((8, 160, 128), F32), 0, 3, (), (0, 1300000))(p3, yr, chat), OCC)
    out = call(
        finish, shape((4, 4, 8, 128), F32), 1, 3, [pltpu.VMEM((128, 128), F32)], (6 * 2 * 256 * 512 * 128, 2000000)
    )(occ, row, r3, chat)
    return out, fits


def allowed(left, right, target):
    return (jnp.bitwise_xor(left, right) == target).astype(F32)


def gather(x, axes, n, dim):
    parts = swap(jnp.broadcast_to(x[None], (n,) + x.shape), axes)
    return jnp.concatenate([parts[p] for p in range(n)], axis=dim)


def dense(t, b, c, occ, vir, aux):
    o, v = occ_at(), vir_at()
    aux_mine = lax.dynamic_slice_in_dim(aux, o * 96, 96)
    vir_mine = lax.dynamic_slice_in_dim(vir, v * 8, 8)
    occ_mine = lax.dynamic_slice_in_dim(occ, o * 4, 4)
    own = b * allowed(vir_mine[None, :, None], vir[None, None, :], aux_mine[:, None, None])
    wide = gather(b, VIR, 16, 1)
    wide = wide * allowed(vir[None, :, None], vir[None, None, :], aux_mine[:, None, None])
    pairs = gather(t, OCC, 8, 1)
    inter = jnp.einsum("qac,qbd->acbd", own, wide, precision=HIGHEST)
    part = jnp.einsum("ijcd,acbd->ijab", gather(pairs, VIR, 16, 2), inter, precision=HIGHEST)
    total = jnp.sum(swap(jnp.moveaxis(part.reshape(4, 8, 4, 8, 128), 1, 0), OCC), axis=0)
    swapped = lax.all_to_all(t, VIR, split_axis=3, concat_axis=2, tiled=True)
    u = 2.0 * t - jnp.transpose(swapped, (0, 1, 3, 2))
    cw = gather(c, VIR, 16, 2)
    cw = cw * allowed(occ_mine[None, :, None], vir[None, None, :], aux[:, None, None])
    part = jnp.einsum("ikac,qkc->iaq", u, cw, precision=HIGHEST)
    y = jnp.sum(swap(jnp.broadcast_to(part[None], (8,) + part.shape), OCC), axis=0)
    return total + jnp.einsum("iaq,qjb->ijab", y, cw, precision=HIGHEST)


def shards(t, b, c, occ, vir, aux):
    fast, fits = folded(t, b, c, occ, vir, aux)
    return lax.cond(fits[0] > 0, lambda *_: fast, dense, t, b, c, occ, vir, aux)


def solution(mesh):
    fine = Mesh(mesh.devices.reshape(2, 4, 4, 2, 2), ("yh", "x", "z", "yl", "core"))
    placed = (P(None, OCC, VIR, None), P(OCC, VIR, None), P(None, OCC, VIR), P(), P(), P())
    return jax.shard_map(shards, mesh=fine, in_specs=placed, out_specs=P(None, OCC, VIR, None), check_vma=False)
```

```python
import functools

import jax
import jax.numpy as jnp
from jax import lax
from jax.experimental import pallas as pl
from jax.experimental.pallas import tpu as pltpu
from jax.sharding import Mesh, PartitionSpec as P

OCC = ("yh", "x")
ZY = ("z", "yl")
VIR = ("z", "yl", "core")
F32 = jnp.float32
BF16 = jnp.bfloat16
HIGHEST = lax.Precision.HIGHEST
SL = 24
SG = 128
NG = 8
VMEM = pl.BlockSpec(memory_space=pltpu.VMEM)
SMEM = pl.BlockSpec(memory_space=pltpu.SMEM)
LIMIT = 14 * 2**20


def occ_at():
    return lax.axis_index("yh") * 4 + lax.axis_index("x")


def vir_at():
    return lax.axis_index("z") * 4 + lax.axis_index("yl") * 2 + lax.axis_index("core")


def iota(shape, dim):
    return lax.broadcasted_iota(jnp.int32, shape, dim)


def split(x):
    hi = x.astype(BF16)
    return hi, (x - hi.astype(F32)).astype(BF16)


def dot(x, y):
    return jnp.dot(x, y, preferred_element_type=F32)


def dot_t(x, y):
    return lax.dot_general(x, y, (((1,), (1,)), ((), ())), preferred_element_type=F32)


def dot3(x, y, product):
    (xh, xl), (yh, yl) = split(x), split(y)
    return product(xh, yh) + product(xh, yl) + product(xl, yh)


def call(body, outs, n_smem, n_vmem, scratch=(), cost=(0, 0), limit=LIMIT):
    return pl.pallas_call(
        body,
        out_shape=outs,
        in_specs=[SMEM] * n_smem + [VMEM] * n_vmem,
        out_specs=jax.tree.map(lambda _: VMEM, outs),
        scratch_shapes=list(scratch),
        compiler_params=pltpu.CompilerParams(vmem_limit_bytes=limit),
        cost_estimate=pl.CostEstimate(flops=cost[0], bytes_accessed=cost[1], transcendentals=0),
    )


def aux_block(aux_ref, block):
    row, skip = lax.div(3 * block, 4), 32 * lax.rem(3 * block, 4)
    first = jnp.broadcast_to(aux_ref[pl.ds(row, 1), :], (8, 128))
    second = jnp.broadcast_to(aux_ref[pl.ds(jnp.minimum(row + 1, 5), 1), :], (8, 128))
    lane = iota((8, 128), 1)
    shift = lax.rem(128 - skip, 128)
    joined = jnp.where(lane < 128 - skip, pltpu.roll(first, shift, 1), pltpu.roll(second, shift, 1))
    return jnp.where(lane < 96, joined, NG)


def aux_blocks(aux_ref):
    rows = jnp.zeros((8, 128), jnp.int32)
    for block in range(8):
        rows = jnp.where(iota((8, 128), 0) == block, aux_block(aux_ref, jnp.int32(block)), rows)
    return rows


def fold_local(vir_s, aux_ref, vir_ref, b_ref, t_ref, out_ref, roll_ref):
    o, v = occ_at(), vir_at()
    q_lane = jnp.broadcast_to(aux_block(aux_ref, o)[0:1], (128, 128))
    q_sub = jnp.transpose(q_lane)
    same = (q_sub == q_lane) & (iota((128, 128), 0) < iota((128, 128), 1))
    rank = jnp.sum(same.astype(F32), axis=0, keepdims=True)
    pick = (rank == iota((SL, 128), 0).astype(F32)).astype(F32)[:, :96].astype(BF16)
    y_row = vir_ref[...]
    for x in range(8):
        keep = (y_row ^ vir_s[v * 8 + x]) == q_sub[:96]
        hi, lo = split(jnp.where(keep, b_ref[:, x, :], 0.0))
        folded = dot(pick, hi) + dot(pick, lo)
        for peer in range(8):
            out_ref[peer, x * SL : (x + 1) * SL, :] = folded
    amps = t_ref[...].reshape(16, 8, 128)
    for k in range(8):
        roll_ref[k] = pltpu.roll(amps, 16 * k, 2) if k else amps
    group = iota((16, 128), 1) // 16
    for peer in range(8):
        block = jnp.zeros((16, 128), F32)
        for c in range(8):
            block = jnp.where(group == c, roll_ref[(c - peer) % 8, :, c, :], block)
        out_ref[peer, 8 * SL : 8 * SL + 16, :] = block


def fold_ov(vir_s, occ_s, aux_ref, c_ref, t_ref, ch_ref, sw_ref, pick_ref, fits_ref):
    o, v = occ_at(), vir_at()
    rows = aux_blocks(aux_ref)
    over = jnp.zeros((8, 1), F32)
    for g in range(NG):
        count = jnp.sum((rows == g).astype(F32), axis=1, keepdims=True)
        over = jnp.maximum(over, jnp.maximum(count - SL, jnp.sum(count, axis=0, keepdims=True) - SG))
    fits_ref[0] = (jnp.max(over) < 0.5).astype(jnp.int32)
    aux = jnp.concatenate([aux_ref[n : n + 1, :] for n in range(6)], axis=1)
    member = (aux == iota((NG, 768), 0)).astype(F32)
    before = (iota((768, 768), 0) < iota((768, 768), 1)).astype(F32).astype(BF16)
    rank = jnp.sum(member * dot(member.astype(BF16), before), axis=0, keepdims=True)
    pick = (rank == iota((SG, 768), 0).astype(F32)).astype(F32).astype(BF16)
    pick_ref[...] = pick
    c_label = jnp.zeros((8, 1), jnp.int32)
    for c in range(8):
        c_label = jnp.where(iota((8, 1), 0) == c, vir_s[v * 8 + c], c_label)
    for k in range(4):
        keep = (c_label ^ occ_s[o * 4 + k]) == aux
        hi, lo = split(jnp.where(keep, c_ref[k], 0.0))
        ch_ref[8 * k : 8 * k + 8, :] = dot_t(hi, pick) + dot_t(lo, pick)
    sw_ref[...] = jnp.transpose(t_ref[...].reshape(128, 128))


def place(aux_ref, place_ref):
    lane = iota((SL, 128), 1).astype(F32) - iota((SL, 128), 0).astype(F32)
    aux = aux_blocks(aux_ref)
    for g in range(NG):
        count = jnp.sum((aux == g).astype(F32), axis=1, keepdims=True)
        start = jnp.zeros((1, 1), F32)
        for block in range(8):
            row = g * 256 + block * SL
            place_ref[row : row + SL, :] = (lane == start).astype(F32)
            start = start + count[block : block + 1, :]
        place_ref[g * 256 + 8 * SL : (g + 1) * 256, :] = jnp.zeros((256 - 8 * SL, 128), F32)


def refold_own(vir_s, aux_ref, vir_ref, r1_ref, ch_ref, sw_ref, out_ref, place_ref, row_ref):
    o, v = occ_at(), vir_at()
    place(aux_ref, place_ref)
    group = iota((1, 128), 1) // 16
    y_row = jnp.broadcast_to(vir_ref[...], (8, 128))
    mine = jnp.zeros((8 * SL, 128), F32)
    label = jnp.zeros((8, 128), jnp.int32)
    for x in range(8):
        shift = lax.rem(16 * x + 128 - 16 * o, 128)
        block = jnp.concatenate([r1_ref[p, x * SL : (x + 1) * SL, :] for p in range(8)], axis=0)
        mine = jnp.where(group == x, pltpu.roll(block, shift, 1), mine)
        label = jnp.where(group == x, pltpu.roll(y_row, shift, 1) ^ vir_s[v * 8 + x], label)
    mine = jnp.transpose(jnp.concatenate([mine, jnp.zeros((256 - 8 * SL, 128), F32)], axis=0))
    label = jnp.transpose(jnp.broadcast_to(label[0:1], (128, 128)))
    label = jnp.concatenate([label, label], axis=1)
    hi, lo = split(mine)
    hi, lo = hi.astype(F32), lo.astype(F32)
    total = jnp.zeros((256, 128), F32)
    for g in range(NG):
        both = jnp.concatenate([jnp.where(label == g, hi, 0.0), jnp.where(label == g, lo, 0.0)], axis=0)
        total = total + dot(both.astype(BF16), place_ref[g * 256 : (g + 1) * 256, :].astype(BF16))
    row_ref[0] = total[:128] + total[128:]
    row_ref[1] = jnp.transpose(
        jnp.concatenate([r1_ref[p, 8 * SL : 8 * SL + 16, :] for p in range(8)], axis=0)
    )
    for d in range(16):
        own = row_ref[0, pl.ds(d, 8, stride=16), :]
        amps = row_ref[1, pl.ds(d, 8, stride=16), :]
        for peer in range(8):
            out_ref[peer, d * 8 : d * 8 + 8, :] = own
            out_ref[peer, 128 + d * 8 : 136 + d * 8, :] = amps
    for peer in range(8):
        out_ref[peer, 256:288, :] = ch_ref[...]
        out_ref[peer, 288:304, :] = sw_ref[16 * peer : 16 * peer + 16, :]


def refold_rows(vir_s, aux_ref, vir_ref, r1_ref, out_ref, place_ref):
    v = vir_at()
    place(aux_ref, place_ref)
    spread = jnp.concatenate(
        [jnp.transpose(place_ref[128 * n : 128 * n + 128, :]).astype(BF16) for n in range(2 * NG)], axis=1
    )
    y_row = vir_ref[...]
    pad = jnp.zeros((256 - 8 * SL, 128), F32)
    for x in range(8):
        label = y_row ^ vir_s[v * 8 + x]
        block = jnp.concatenate([r1_ref[p, x * SL : (x + 1) * SL, :] for p in range(8)] + [pad], axis=0)
        hi, lo = split(block)
        both = jnp.concatenate([hi, lo], axis=1)
        total = jnp.zeros((SG, 256), F32)
        for g in range(NG):
            keep = (label == g).astype(F32)
            keep = jnp.concatenate([keep, keep], axis=1).astype(BF16)
            total = total + dot(spread[:, g * 256 : (g + 1) * 256], both * keep)
        hi, lo = split(total[:, :128] + total[:, 128:])
        out_ref[0:128, x * 128 : x * 128 + 128] = hi
        out_ref[128:256, x * 128 : x * 128 + 128] = lo
        out_ref[256:384, x * 128 : x * 128 + 128] = hi


def cycle_first(occ_s, vir_ref, r2_ref, o2_ref, t_ref, pick_ref, aux_ref, y_ref, chat_ref, f_ref, amps_ref, got_ref):
    o, core = occ_at(), lax.axis_index("core")
    for ref, part in ((r2_ref, core), (o2_ref, 1 - core)):
        for p in range(8):
            f_ref[:, 2 * p + part] = ref[p, 0:128, :].reshape(16, 8, 128)
            amps_ref[:, 2 * p + part] = ref[p, 128:256, :].reshape(16, 8, 128)
    for p in range(8):
        got_ref[2 * p + core] = r2_ref[p, 256:304, :]
        got_ref[2 * p + 1 - core] = o2_ref[p, 256:304, :]
    for k in range(4):
        for n in range(16):
            chat_ref[k * 128 + n * 8 : k * 128 + n * 8 + 8, :] = got_ref[n, 8 * k : 8 * k + 8, :]
    group = iota((8, 128), 1) // 8
    blocks = [got_ref[n, pl.ds(pl.multiple_of(32 + 8 * core, 8), 8), :] for n in range(16)]
    u = []
    for i in range(4):
        row = []
        for k in range(4):
            swapped = jnp.zeros((8, 128), F32)
            for n in range(16):
                shift = (8 * (n - 4 * i - k)) % 128
                swapped = jnp.where(group == n, pltpu.roll(blocks[n], shift, 1) if shift else blocks[n], swapped)
            row.append(2.0 * t_ref[i, k] - swapped)
        u.append(jnp.concatenate(row, axis=1))
    u = jnp.concatenate(u, axis=0)
    label = jnp.concatenate([vir_ref[...] ^ occ_s[o * 4 + k] for k in range(4)], axis=1)
    rows = jnp.concatenate([jnp.where(label == g, u, 0.0) for g in range(NG)], axis=0)
    hi, lo = split(dot3(rows, chat_ref[...], dot))
    y = dot(hi, pick_ref[...]) + dot(lo, pick_ref[...])
    for n in range(6):
        aux = aux_ref[n : n + 1, :]
        part = jnp.zeros((32, 128), F32)
        for g in range(NG):
            part = jnp.where(aux == g, y[32 * g : 32 * g + 32, 128 * n : 128 * n + 128], part)
        y_ref[32 * n : 32 * n + 32, :] = part


def ladder(vir_s, vir_ref, b1_ref, f_ref, t_ref, y_ref, out_ref, hi_ref, lo_ref, acc_ref):
    o, v = occ_at(), vir_at()
    acc_ref[...] = jnp.zeros_like(acc_ref)
    c_lane = jnp.broadcast_to(vir_ref[...], (128, 128))
    bc = jnp.transpose(c_lane) ^ c_lane

    def step(n, carry):
        amps = []
        for half in range(2):
            d = 2 * n + half
            hi, lo = split(f_ref[d].reshape(128, 128))
            w = dot(jnp.concatenate([hi, hi, lo], axis=1), b1_ref[...])
            d_label = vir_s[o * 16 + d]
            for a in range(8):
                keep = bc == (vir_s[v * 8 + a] ^ d_label)
                hi, lo = split(jnp.where(keep, w[:, a * 128 : a * 128 + 128], 0.0))
                hi_ref[a * 128 : a * 128 + 128, half * 128 : half * 128 + 128] = hi
                lo_ref[a * 128 : a * 128 + 128, half * 128 : half * 128 + 128] = lo
            amps.append(t_ref[d].reshape(128, 128))
        hi, lo = split(jnp.concatenate(amps, axis=0))
        r = dot(hi_ref[...], jnp.concatenate([hi, lo], axis=1))
        acc_ref[...] += r[:, :128] + r[:, 128:] + dot(lo_ref[...], hi)
        return carry

    lax.fori_loop(0, 8, step, 0, unroll=True)
    for a in range(8):
        rows = jnp.transpose(acc_ref[a * 128 : a * 128 + 128, :])
        for p in range(8):
            out_ref[p, 16 * a : 16 * a + 16, :] = rows[16 * p : 16 * p + 16, :]
    for p in range(8):
        out_ref[p, 128:320, :] = y_ref[...]


def finish(occ_s, vir_ref, r3_ref, chat_ref, pick_ref, aux_ref, out_ref, sum_ref):
    o = occ_at()
    total = r3_ref[0]
    for p in range(1, 8):
        total = total + r3_ref[p]
    sum_ref[...] = total[0:128]
    y = jnp.concatenate([total[128 + 32 * n : 160 + 32 * n] for n in range(6)], axis=1)
    aux = jnp.concatenate([aux_ref[n : n + 1, :] for n in range(6)], axis=1)
    hi, lo = split(jnp.concatenate([jnp.where(aux == g, y, 0.0) for g in range(NG)], axis=0))
    z = dot3(dot_t(hi, pick_ref[...]) + dot_t(lo, pick_ref[...]), chat_ref[...], dot_t)
    for j in range(4):
        label = vir_ref[...] ^ occ_s[o * 4 + j]
        part = jnp.zeros((32, 128), F32)
        for g in range(NG):
            part = jnp.where(label == g, z[g * 32 : g * 32 + 32, j * 128 : j * 128 + 128], part)
        for i in range(4):
            out_ref[i, j] = sum_ref[pl.ds(i * 4 + j, 8, stride=16), :] + part[8 * i : 8 * i + 8, :]


def swap(x, axes):
    return lax.all_to_all(x, axes, 0, 0, tiled=True)


def folded(t, b, c, occ, vir, aux):
    aux, row = aux.reshape(6, 128), vir.reshape(1, 128)
    shape = jax.ShapeDtypeStruct
    p1 = call(
        fold_local, shape((8, 8 * SL + 16, 128), F32), 1, 4, [pltpu.VMEM((8, 16, 8, 128), F32)],
        (2 * 2 * 24 * 96 * 1024, 1300000), 56 * 2**20,
    )(vir, aux, row, b, t)
    r1 = swap(p1, OCC)
    ch, sw, pick, fits = pl.pallas_call(
        fold_ov,
        out_shape=(shape((32, 128), F32), shape((128, 128), F32), shape((SG, 768), BF16), shape((1,), jnp.int32)),
        in_specs=[SMEM, SMEM, VMEM, VMEM, VMEM],
        out_specs=(VMEM, VMEM, VMEM, SMEM),
        compiler_params=pltpu.CompilerParams(vmem_limit_bytes=LIMIT),
        cost_estimate=pl.CostEstimate(flops=2 * 8 * 768 * 768, bytes_accessed=300000, transcendentals=0),
    )(vir, occ, aux, jnp.transpose(c, (1, 2, 0)), t)
    p2 = call(
        refold_own, shape((8, 304, 128), F32), 1, 5, [pltpu.VMEM((2048, 128), F32), pltpu.VMEM((2, 128, 128), F32)],
        (2 * 256 * 2048 * 128, 2300000),
    )(vir, aux, row, r1, ch, sw)
    r2 = swap(p2, ZY)
    b1 = call(
        refold_rows, shape((384, 1024), BF16), 1, 3, [pltpu.VMEM((2048, 128), F32)], (2 * 128 * 2048 * 2048, 1700000)
    )(vir, aux, row, r1)
    o2 = lax.ppermute(r2, "core", [(0, 1), (1, 0)])
    staged = shape((16, 16, 8, 128), F32)
    y, chat, f, amps = call(
        cycle_first, (shape((192, 128), F32), shape((512, 128), F32), staged, staged), 1, 6,
        [pltpu.VMEM((16, 48, 128), F32)], (6 * 2 * 256 * 512 * 128, 4000000),
    )(occ, row, r2, o2, t, pick, aux)
    p3 = call(
        ladder, shape((8, 320, 128), F32), 1, 5,
        [pltpu.VMEM((1024, 256), BF16), pltpu.VMEM((1024, 256), BF16), pltpu.VMEM((1024, 128), F32)],
        (6 * 2048 * 1024 * 256, 4000000),
    )(vir, row, b1, f, amps, y)
    r3 = swap(p3, OCC)
    out = call(
        finish, shape((4, 4, 8, 128), F32), 1, 5, [pltpu.VMEM((128, 128), F32)], (6 * 2 * 256 * 512 * 128, 2000000)
    )(occ, row, r3, chat, pick, aux)
    return out, fits


def allowed(left, right, target):
    return (jnp.bitwise_xor(left, right) == target).astype(F32)


def gather(x, axes, n, dim):
    parts = swap(jnp.broadcast_to(x[None], (n,) + x.shape), axes)
    return jnp.concatenate([parts[p] for p in range(n)], axis=dim)


def dense(t, b, c, occ, vir, aux):
    o, v = occ_at(), vir_at()
    aux_mine = lax.dynamic_slice_in_dim(aux, o * 96, 96)
    vir_mine = lax.dynamic_slice_in_dim(vir, v * 8, 8)
    occ_mine = lax.dynamic_slice_in_dim(occ, o * 4, 4)
    own = b * allowed(vir_mine[None, :, None], vir[None, None, :], aux_mine[:, None, None])
    wide = gather(b, VIR, 16, 1)
    wide = wide * allowed(vir[None, :, None], vir[None, None, :], aux_mine[:, None, None])
    pairs = gather(t, OCC, 8, 1)
    inter = jnp.einsum("qac,qbd->acbd", own, wide, precision=HIGHEST)
    part = jnp.einsum("ijcd,acbd->ijab", gather(pairs, VIR, 16, 2), inter, precision=HIGHEST)
    total = jnp.sum(swap(jnp.moveaxis(part.reshape(4, 8, 4, 8, 128), 1, 0), OCC), axis=0)
    swapped = lax.all_to_all(t, VIR, split_axis=3, concat_axis=2, tiled=True)
    u = 2.0 * t - jnp.transpose(swapped, (0, 1, 3, 2))
    cw = gather(c, VIR, 16, 2)
    cw = cw * allowed(occ_mine[None, :, None], vir[None, None, :], aux[:, None, None])
    part = jnp.einsum("ikac,qkc->iaq", u, cw, precision=HIGHEST)
    y = jnp.sum(swap(jnp.broadcast_to(part[None], (8,) + part.shape), OCC), axis=0)
    return total + jnp.einsum("iaq,qjb->ijab", y, cw, precision=HIGHEST)


def shards(t, b, c, occ, vir, aux):
    fast, fits = folded(t, b, c, occ, vir, aux)
    return lax.cond(fits[0] > 0, lambda *_: fast, dense, t, b, c, occ, vir, aux)


def solution(mesh):
    fine = Mesh(mesh.devices.reshape(2, 4, 4, 2, 2), ("yh", "x", "z", "yl", "core"))
    placed = (P(None, OCC, VIR, None), P(OCC, VIR, None), P(None, OCC, VIR), P(), P(), P())
    return jax.shard_map(shards, mesh=fine, in_specs=placed, out_specs=P(None, OCC, VIR, None), check_vma=False)
```

```python
import functools

import jax
import jax.numpy as jnp
from jax import lax
from jax.experimental import pallas as pl
from jax.experimental.pallas import tpu as pltpu
from jax.sharding import Mesh, PartitionSpec as P

OCC = ("yh", "x")
ZY = ("z", "yl")
VIR = ("z", "yl", "core")
F32 = jnp.float32
BF16 = jnp.bfloat16
HIGHEST = lax.Precision.HIGHEST
SL = 24
SG = 128
NG = 8
VMEM = pl.BlockSpec(memory_space=pltpu.VMEM)
SMEM = pl.BlockSpec(memory_space=pltpu.SMEM)
LIMIT = 14 * 2**20


def occ_at():
    return lax.axis_index("yh") * 4 + lax.axis_index("x")


def vir_at():
    return lax.axis_index("z") * 4 + lax.axis_index("yl") * 2 + lax.axis_index("core")


def iota(shape, dim):
    return lax.broadcasted_iota(jnp.int32, shape, dim)


def split(x):
    hi = x.astype(BF16)
    return hi, (x - hi.astype(F32)).astype(BF16)


def dot(x, y):
    return jnp.dot(x, y, preferred_element_type=F32)


def dot_t(x, y):
    return lax.dot_general(x, y, (((1,), (1,)), ((), ())), preferred_element_type=F32)


def dot3(x, y, product):
    (xh, xl), (yh, yl) = split(x), split(y)
    return product(xh, yh) + product(xh, yl) + product(xl, yh)


def call(body, outs, n_smem, n_vmem, scratch=(), cost=(0, 0), limit=LIMIT):
    return pl.pallas_call(
        body,
        out_shape=outs,
        in_specs=[SMEM] * n_smem + [VMEM] * n_vmem,
        out_specs=jax.tree.map(lambda _: VMEM, outs),
        scratch_shapes=list(scratch),
        compiler_params=pltpu.CompilerParams(vmem_limit_bytes=limit),
        cost_estimate=pl.CostEstimate(flops=cost[0], bytes_accessed=cost[1], transcendentals=0),
    )


def aux_block(aux_ref, block):
    row, skip = lax.div(3 * block, 4), 32 * lax.rem(3 * block, 4)
    first = jnp.broadcast_to(aux_ref[pl.ds(row, 1), :], (8, 128))
    second = jnp.broadcast_to(aux_ref[pl.ds(jnp.minimum(row + 1, 5), 1), :], (8, 128))
    lane = iota((8, 128), 1)
    shift = lax.rem(128 - skip, 128)
    joined = jnp.where(lane < 128 - skip, pltpu.roll(first, shift, 1), pltpu.roll(second, shift, 1))
    return jnp.where(lane < 96, joined, NG)


def aux_blocks(aux_ref):
    rows = jnp.zeros((8, 128), jnp.int32)
    for block in range(8):
        rows = jnp.where(iota((8, 128), 0) == block, aux_block(aux_ref, jnp.int32(block)), rows)
    return rows


def fold_local(vir_s, aux_ref, vir_ref, b_ref, t_ref, out_ref, roll_ref):
    o, v = occ_at(), vir_at()
    q_lane = jnp.broadcast_to(aux_block(aux_ref, o)[0:1], (128, 128))
    q_sub = jnp.transpose(q_lane)
    same = (q_sub == q_lane) & (iota((128, 128), 0) < iota((128, 128), 1))
    rank = jnp.sum(same.astype(F32), axis=0, keepdims=True)
    pick = (rank == iota((SL, 128), 0).astype(F32)).astype(F32)[:, :96].astype(BF16)
    y_row = vir_ref[...]
    for x in range(8):
        keep = (y_row ^ vir_s[v * 8 + x]) == q_sub[:96]
        hi, lo = split(jnp.where(keep, b_ref[:, x, :], 0.0))
        folded = dot(pick, hi) + dot(pick, lo)
        for peer in range(8):
            out_ref[peer, x * SL : (x + 1) * SL, :] = folded
    amps = t_ref[...].reshape(16, 8, 128)
    for k in range(8):
        roll_ref[k] = pltpu.roll(amps, 16 * k, 2) if k else amps
    group = iota((16, 128), 1) // 16
    for peer in range(8):
        block = jnp.zeros((16, 128), F32)
        for c in range(8):
            block = jnp.where(group == c, roll_ref[(c - peer) % 8, :, c, :], block)
        out_ref[peer, 8 * SL : 8 * SL + 16, :] = block


def fold_ov(vir_s, occ_s, aux_ref, c_ref, t_ref, ch_ref, sw_ref, pick_ref, fits_ref):
    o, v = occ_at(), vir_at()
    rows = aux_blocks(aux_ref)
    over = jnp.zeros((8, 1), F32)
    for g in range(NG):
        count = jnp.sum((rows == g).astype(F32), axis=1, keepdims=True)
        over = jnp.maximum(over, jnp.maximum(count - SL, jnp.sum(count, axis=0, keepdims=True) - SG))
    fits_ref[0] = (jnp.max(over) < 0.5).astype(jnp.int32)
    aux = jnp.concatenate([aux_ref[n : n + 1, :] for n in range(6)], axis=1)
    member = (aux == iota((NG, 768), 0)).astype(F32)
    before = (iota((768, 768), 0) < iota((768, 768), 1)).astype(F32).astype(BF16)
    rank = jnp.sum(member * dot(member.astype(BF16), before), axis=0, keepdims=True)
    pick = (rank == iota((SG, 768), 0).astype(F32)).astype(F32).astype(BF16)
    pick_ref[...] = pick
    c_label = jnp.zeros((8, 1), jnp.int32)
    for c in range(8):
        c_label = jnp.where(iota((8, 1), 0) == c, vir_s[v * 8 + c], c_label)
    for k in range(4):
        keep = (c_label ^ occ_s[o * 4 + k]) == aux
        hi, lo = split(jnp.where(keep, c_ref[k], 0.0))
        ch_ref[8 * k : 8 * k + 8, :] = dot_t(hi, pick) + dot_t(lo, pick)
    sw_ref[...] = jnp.transpose(t_ref[...].reshape(128, 128))


def place(aux_ref, place_ref):
    lane = iota((SL, 128), 1).astype(F32) - iota((SL, 128), 0).astype(F32)
    aux = aux_blocks(aux_ref)
    for g in range(NG):
        count = jnp.sum((aux == g).astype(F32), axis=1, keepdims=True)
        start = jnp.zeros((1, 1), F32)
        for block in range(8):
            row = g * 256 + block * SL
            place_ref[row : row + SL, :] = (lane == start).astype(F32)
            start = start + count[block : block + 1, :]
        place_ref[g * 256 + 8 * SL : (g + 1) * 256, :] = jnp.zeros((256 - 8 * SL, 128), F32)


def refold_own(vir_s, aux_ref, vir_ref, r1_ref, ch_ref, sw_ref, out_ref, place_ref, row_ref):
    o, v = occ_at(), vir_at()
    place(aux_ref, place_ref)
    group = iota((1, 128), 1) // 16
    y_row = jnp.broadcast_to(vir_ref[...], (8, 128))
    mine = jnp.zeros((8 * SL, 128), F32)
    label = jnp.zeros((8, 128), jnp.int32)
    for x in range(8):
        shift = lax.rem(16 * x + 128 - 16 * o, 128)
        block = jnp.concatenate([r1_ref[p, x * SL : (x + 1) * SL, :] for p in range(8)], axis=0)
        mine = jnp.where(group == x, pltpu.roll(block, shift, 1), mine)
        label = jnp.where(group == x, pltpu.roll(y_row, shift, 1) ^ vir_s[v * 8 + x], label)
    mine = jnp.transpose(jnp.concatenate([mine, jnp.zeros((256 - 8 * SL, 128), F32)], axis=0))
    label = jnp.transpose(jnp.broadcast_to(label[0:1], (128, 128)))
    label = jnp.concatenate([label, label], axis=1)
    hi, lo = split(mine)
    hi, lo = hi.astype(F32), lo.astype(F32)
    total = jnp.zeros((256, 128), F32)
    for g in range(NG):
        both = jnp.concatenate([jnp.where(label == g, hi, 0.0), jnp.where(label == g, lo, 0.0)], axis=0)
        total = total + dot(both.astype(BF16), place_ref[g * 256 : (g + 1) * 256, :].astype(BF16))
    row_ref[0] = total[:128] + total[128:]
    row_ref[1] = jnp.transpose(
        jnp.concatenate([r1_ref[p, 8 * SL : 8 * SL + 16, :] for p in range(8)], axis=0)
    )
    for d in range(16):
        own = row_ref[0, pl.ds(d, 8, stride=16), :]
        amps = row_ref[1, pl.ds(d, 8, stride=16), :]
        for peer in range(8):
            out_ref[peer, d * 8 : d * 8 + 8, :] = own
            out_ref[peer, 128 + d * 8 : 136 + d * 8, :] = amps
    for peer in range(8):
        out_ref[peer, 256:288, :] = ch_ref[...]
        out_ref[peer, 288:304, :] = sw_ref[16 * peer : 16 * peer + 16, :]


def refold_rows(vir_s, aux_ref, vir_ref, r1_ref, out_ref, place_ref):
    v = vir_at()
    place(aux_ref, place_ref)
    spread = jnp.concatenate(
        [jnp.transpose(place_ref[128 * n : 128 * n + 128, :]).astype(BF16) for n in range(2 * NG)], axis=1
    )
    y_row = vir_ref[...]
    pad = jnp.zeros((256 - 8 * SL, 128), F32)
    for x in range(8):
        label = y_row ^ vir_s[v * 8 + x]
        block = jnp.concatenate([r1_ref[p, x * SL : (x + 1) * SL, :] for p in range(8)] + [pad], axis=0)
        hi, lo = split(block)
        both = jnp.concatenate([hi, lo], axis=1)
        total = jnp.zeros((SG, 256), F32)
        for g in range(NG):
            keep = (label == g).astype(F32)
            keep = jnp.concatenate([keep, keep], axis=1).astype(BF16)
            total = total + dot(spread[:, g * 256 : (g + 1) * 256], both * keep)
        hi, lo = split(total[:, :128] + total[:, 128:])
        out_ref[0:128, x * 128 : x * 128 + 128] = hi
        out_ref[128:256, x * 128 : x * 128 + 128] = lo
        out_ref[256:384, x * 128 : x * 128 + 128] = hi


def cycle_first(occ_s, vir_ref, r2_ref, o2_ref, t_ref, pick_ref, aux_ref, y_ref, chat_ref, f_ref, amps_ref, got_ref):
    o, core = occ_at(), lax.axis_index("core")
    for ref, part in ((r2_ref, core), (o2_ref, 1 - core)):
        for p in range(8):
            f_ref[:, 2 * p + part] = ref[p, 0:128, :].reshape(16, 8, 128)
            amps_ref[:, 2 * p + part] = ref[p, 128:256, :].reshape(16, 8, 128)
    for p in range(8):
        got_ref[2 * p + core] = r2_ref[p, 256:304, :]
        got_ref[2 * p + 1 - core] = o2_ref[p, 256:304, :]
    for k in range(4):
        for n in range(16):
            chat_ref[k * 128 + n * 8 : k * 128 + n * 8 + 8, :] = got_ref[n, 8 * k : 8 * k + 8, :]
    group = iota((8, 128), 1) // 8
    blocks = [got_ref[n, pl.ds(pl.multiple_of(32 + 8 * core, 8), 8), :] for n in range(16)]
    u = []
    for i in range(4):
        row = []
        for k in range(4):
            swapped = jnp.zeros((8, 128), F32)
            for n in range(16):
                shift = (8 * (n - 4 * i - k)) % 128
                swapped = jnp.where(group == n, pltpu.roll(blocks[n], shift, 1) if shift else blocks[n], swapped)
            row.append(2.0 * t_ref[i, k] - swapped)
        u.append(jnp.concatenate(row, axis=1))
    u = jnp.concatenate(u, axis=0)
    label = jnp.concatenate([vir_ref[...] ^ occ_s[o * 4 + k] for k in range(4)], axis=1)
    rows = jnp.concatenate([jnp.where(label == g, u, 0.0) for g in range(NG)], axis=0)
    hi, lo = split(dot3(rows, chat_ref[...], dot))
    y = dot(hi, pick_ref[...]) + dot(lo, pick_ref[...])
    for n in range(6):
        aux = aux_ref[n : n + 1, :]
        part = jnp.zeros((32, 128), F32)
        for g in range(NG):
            part = jnp.where(aux == g, y[32 * g : 32 * g + 32, 128 * n : 128 * n + 128], part)
        y_ref[32 * n : 32 * n + 32, :] = part


def ladder(vir_s, vir_ref, b1_ref, f_ref, t_ref, y_ref, out_ref, hi_ref, lo_ref, acc_ref):
    o, v = occ_at(), vir_at()
    acc_ref[...] = jnp.zeros_like(acc_ref)
    c_lane = jnp.broadcast_to(vir_ref[...], (128, 128))
    bc = jnp.transpose(c_lane) ^ c_lane

    def step(n, carry):
        amps = []
        for half in range(2):
            d = 2 * n + half
            hi, lo = split(f_ref[d].reshape(128, 128))
            w = dot(jnp.concatenate([hi, hi, lo], axis=1), b1_ref[...])
            d_label = vir_s[o * 16 + d]
            for a in range(8):
                keep = bc == (vir_s[v * 8 + a] ^ d_label)
                hi, lo = split(jnp.where(keep, w[:, a * 128 : a * 128 + 128], 0.0))
                hi_ref[a * 128 : a * 128 + 128, half * 128 : half * 128 + 128] = hi
                lo_ref[a * 128 : a * 128 + 128, half * 128 : half * 128 + 128] = lo
            amps.append(t_ref[d].reshape(128, 128))
        hi, lo = split(jnp.concatenate(amps, axis=0))
        r = dot(hi_ref[...], jnp.concatenate([hi, lo], axis=1))
        acc_ref[...] += r[:, :128] + r[:, 128:] + dot(lo_ref[...], hi)
        return carry

    lax.fori_loop(0, 8, step, 0, unroll=True)
    for a in range(8):
        rows = jnp.transpose(acc_ref[a * 128 : a * 128 + 128, :])
        for p in range(8):
            out_ref[p, 16 * a : 16 * a + 16, :] = rows[16 * p : 16 * p + 16, :]
    for p in range(8):
        out_ref[p, 128:320, :] = y_ref[...]


def cycle_and_ladder(
    vir_s, occ_s, vir_ref, aux_ref, r2_ref, o2_ref, t_ref, pick_ref, b1_ref, out_ref, chat_ref,
    y_ref, f_ref, amps_ref, got_ref, hi_ref, lo_ref, acc_ref,
):
    cycle_first(occ_s, vir_ref, r2_ref, o2_ref, t_ref, pick_ref, aux_ref, y_ref, chat_ref, f_ref, amps_ref, got_ref)
    ladder(vir_s, vir_ref, b1_ref, f_ref, amps_ref, y_ref, out_ref, hi_ref, lo_ref, acc_ref)


def unfold(occ_s, vir_ref, chat_ref, pick_ref, aux_ref, hi_ref, lo_ref):
    o = occ_at()
    aux = jnp.concatenate([aux_ref[n : n + 1, :] for n in range(6)], axis=1)
    label = jnp.transpose(jnp.broadcast_to(vir_ref[...], (128, 128)))[:, :1]
    for j in range(4):
        hi, lo = split(chat_ref[128 * j : 128 * j + 128, :])
        wide = dot(hi, pick_ref[...]) + dot(lo, pick_ref[...])
        hi, lo = split(jnp.where((label ^ occ_s[o * 4 + j]) == aux, wide, 0.0))
        hi_ref[128 * j : 128 * j + 128, :] = hi
        lo_ref[128 * j : 128 * j + 128, :] = lo


def finish(r3_ref, ch_ref, cl_ref, out_ref, sum_ref):
    total = r3_ref[0]
    for p in range(1, 8):
        total = total + r3_ref[p]
    sum_ref[...] = total[0:128]
    hi, lo = split(jnp.concatenate([total[128 + 32 * n : 160 + 32 * n] for n in range(6)], axis=1))
    z = dot_t(hi, ch_ref[...]) + dot_t(hi, cl_ref[...]) + dot_t(lo, ch_ref[...])
    for i in range(4):
        for j in range(4):
            part = z[8 * i : 8 * i + 8, 128 * j : 128 * j + 128]
            out_ref[i, j] = sum_ref[pl.ds(i * 4 + j, 8, stride=16), :] + part


def swap(x, axes):
    return lax.all_to_all(x, axes, 0, 0, tiled=True)


def folded(t, b, c, occ, vir, aux):
    aux, row = aux.reshape(6, 128), vir.reshape(1, 128)
    shape = jax.ShapeDtypeStruct
    p1 = call(
        fold_local, shape((8, 8 * SL + 16, 128), F32), 1, 4, [pltpu.VMEM((8, 16, 8, 128), F32)],
        (2 * 2 * 24 * 96 * 1024, 1300000), 56 * 2**20,
    )(vir, aux, row, b, t)
    r1 = swap(p1, OCC)
    ch, sw, pick, fits = pl.pallas_call(
        fold_ov,
        out_shape=(shape((32, 128), F32), shape((128, 128), F32), shape((SG, 768), BF16), shape((1,), jnp.int32)),
        in_specs=[SMEM, SMEM, VMEM, VMEM, VMEM],
        out_specs=(VMEM, VMEM, VMEM, SMEM),
        compiler_params=pltpu.CompilerParams(vmem_limit_bytes=LIMIT),
        cost_estimate=pl.CostEstimate(flops=2 * 8 * 768 * 768, bytes_accessed=300000, transcendentals=0),
    )(vir, occ, aux, jnp.transpose(c, (1, 2, 0)), t)
    p2 = call(
        refold_own, shape((8, 304, 128), F32), 1, 5, [pltpu.VMEM((2048, 128), F32), pltpu.VMEM((2, 128, 128), F32)],
        (2 * 256 * 2048 * 128, 2300000),
    )(vir, aux, row, r1, ch, sw)
    r2 = swap(p2, ZY)
    b1 = call(
        refold_rows, shape((384, 1024), BF16), 1, 3, [pltpu.VMEM((2048, 128), F32)], (2 * 128 * 2048 * 2048, 1700000)
    )(vir, aux, row, r1)
    o2 = lax.ppermute(r2, "core", [(0, 1), (1, 0)])
    staged = (16, 16, 8, 128)
    p3, chat = call(
        cycle_and_ladder, (shape((8, 320, 128), F32), shape((512, 128), F32)), 2, 7,
        [
            pltpu.VMEM((192, 128), F32),
            pltpu.VMEM(staged, F32),
            pltpu.VMEM(staged, F32),
            pltpu.VMEM((16, 48, 128), F32),
            pltpu.VMEM((1024, 256), BF16),
            pltpu.VMEM((1024, 256), BF16),
            pltpu.VMEM((1024, 128), F32),
        ],
        (6 * 2048 * 1024 * 256 + 6 * 2 * 256 * 512 * 128, 5000000),
    )(vir, occ, row, aux, r2, o2, t, pick, b1)
    r3 = swap(p3, OCC)
    ch, cl = call(
        unfold, (shape((512, 768), BF16), shape((512, 768), BF16)), 1, 4, (), (4 * 512 * 768 * 128, 2000000)
    )(occ, row, chat, pick, aux)
    out = call(
        finish, shape((4, 4, 8, 128), F32), 0, 3, [pltpu.VMEM((128, 128), F32)], (6 * 32 * 512 * 768, 3000000)
    )(r3, ch, cl)
    return out, fits


def allowed(left, right, target):
    return (jnp.bitwise_xor(left, right) == target).astype(F32)


def gather(x, axes, n, dim):
    parts = swap(jnp.broadcast_to(x[None], (n,) + x.shape), axes)
    return jnp.concatenate([parts[p] for p in range(n)], axis=dim)


def dense(t, b, c, occ, vir, aux):
    o, v = occ_at(), vir_at()
    aux_mine = lax.dynamic_slice_in_dim(aux, o * 96, 96)
    vir_mine = lax.dynamic_slice_in_dim(vir, v * 8, 8)
    occ_mine = lax.dynamic_slice_in_dim(occ, o * 4, 4)
    own = b * allowed(vir_mine[None, :, None], vir[None, None, :], aux_mine[:, None, None])
    wide = gather(b, VIR, 16, 1)
    wide = wide * allowed(vir[None, :, None], vir[None, None, :], aux_mine[:, None, None])
    pairs = gather(t, OCC, 8, 1)
    inter = jnp.einsum("qac,qbd->acbd", own, wide, precision=HIGHEST)
    part = jnp.einsum("ijcd,acbd->ijab", gather(pairs, VIR, 16, 2), inter, precision=HIGHEST)
    total = jnp.sum(swap(jnp.moveaxis(part.reshape(4, 8, 4, 8, 128), 1, 0), OCC), axis=0)
    swapped = lax.all_to_all(t, VIR, split_axis=3, concat_axis=2, tiled=True)
    u = 2.0 * t - jnp.transpose(swapped, (0, 1, 3, 2))
    cw = gather(c, VIR, 16, 2)
    cw = cw * allowed(occ_mine[None, :, None], vir[None, None, :], aux[:, None, None])
    part = jnp.einsum("ikac,qkc->iaq", u, cw, precision=HIGHEST)
    y = jnp.sum(swap(jnp.broadcast_to(part[None], (8,) + part.shape), OCC), axis=0)
    return total + jnp.einsum("iaq,qjb->ijab", y, cw, precision=HIGHEST)


def shards(t, b, c, occ, vir, aux):
    fast, fits = folded(t, b, c, occ, vir, aux)
    return lax.cond(fits[0] > 0, lambda *_: fast, dense, t, b, c, occ, vir, aux)


def solution(mesh):
    fine = Mesh(mesh.devices.reshape(2, 4, 4, 2, 2), ("yh", "x", "z", "yl", "core"))
    placed = (P(None, OCC, VIR, None), P(OCC, VIR, None), P(None, OCC, VIR), P(), P(), P())
    return jax.shard_map(shards, mesh=fine, in_specs=placed, out_specs=P(None, OCC, VIR, None), check_vma=False)
```

```python
import functools

import jax
import jax.numpy as jnp
from jax import lax
from jax.experimental import pallas as pl
from jax.experimental.pallas import tpu as pltpu
from jax.sharding import Mesh, PartitionSpec as P

OCC = ("yh", "x")
ZY = ("z", "yl")
VIR = ("z", "yl", "core")
F32 = jnp.float32
BF16 = jnp.bfloat16
HIGHEST = lax.Precision.HIGHEST
SL = 24
SG = 128
NG = 8
VMEM = pl.BlockSpec(memory_space=pltpu.VMEM)
SMEM = pl.BlockSpec(memory_space=pltpu.SMEM)
LIMIT = 14 * 2**20


def occ_at():
    return lax.axis_index("yh") * 4 + lax.axis_index("x")


def vir_at():
    return lax.axis_index("z") * 4 + lax.axis_index("yl") * 2 + lax.axis_index("core")


def iota(shape, dim):
    return lax.broadcasted_iota(jnp.int32, shape, dim)


def split(x):
    hi = x.astype(BF16)
    return hi, (x - hi.astype(F32)).astype(BF16)


def dot(x, y):
    return jnp.dot(x, y, preferred_element_type=F32)


def dot_t(x, y):
    return lax.dot_general(x, y, (((1,), (1,)), ((), ())), preferred_element_type=F32)


def dot3(x, y, product):
    (xh, xl), (yh, yl) = split(x), split(y)
    return product(xh, yh) + product(xh, yl) + product(xl, yh)


def call(body, outs, n_smem, n_vmem, scratch=(), cost=(0, 0), limit=LIMIT):
    return pl.pallas_call(
        body,
        out_shape=outs,
        in_specs=[SMEM] * n_smem + [VMEM] * n_vmem,
        out_specs=jax.tree.map(lambda _: VMEM, outs),
        scratch_shapes=list(scratch),
        compiler_params=pltpu.CompilerParams(vmem_limit_bytes=limit),
        cost_estimate=pl.CostEstimate(flops=cost[0], bytes_accessed=cost[1], transcendentals=0),
    )


def aux_block(aux_ref, block):
    row, skip = lax.div(3 * block, 4), 32 * lax.rem(3 * block, 4)
    first = jnp.broadcast_to(aux_ref[pl.ds(row, 1), :], (8, 128))
    second = jnp.broadcast_to(aux_ref[pl.ds(jnp.minimum(row + 1, 5), 1), :], (8, 128))
    lane = iota((8, 128), 1)
    shift = lax.rem(128 - skip, 128)
    joined = jnp.where(lane < 128 - skip, pltpu.roll(first, shift, 1), pltpu.roll(second, shift, 1))
    return jnp.where(lane < 96, joined, NG)


def aux_blocks(aux_ref):
    rows = jnp.zeros((8, 128), jnp.int32)
    for block in range(8):
        rows = jnp.where(iota((8, 128), 0) == block, aux_block(aux_ref, jnp.int32(block)), rows)
    return rows


def fold_local(vir_s, aux_ref, vir_ref, b_ref, t_ref, out_ref, roll_ref):
    o, v = occ_at(), vir_at()
    q_lane = jnp.broadcast_to(aux_block(aux_ref, o)[0:1], (128, 128))
    q_sub = jnp.transpose(q_lane)
    same = (q_sub == q_lane) & (iota((128, 128), 0) < iota((128, 128), 1))
    rank = jnp.sum(same.astype(F32), axis=0, keepdims=True)
    pick = (rank == iota((SL, 128), 0).astype(F32)).astype(F32)[:, :96].astype(BF16)
    y_row = vir_ref[...]
    for x in range(8):
        keep = (y_row ^ vir_s[v * 8 + x]) == q_sub[:96]
        hi, lo = split(jnp.where(keep, b_ref[:, x, :], 0.0))
        both = dot(pick, jnp.concatenate([hi, lo], axis=1))
        folded = both[:, :128] + both[:, 128:]
        for peer in range(8):
            out_ref[peer, x * SL : (x + 1) * SL, :] = folded
    amps = t_ref[...].reshape(16, 8, 128)
    for k in range(8):
        roll_ref[k] = pltpu.roll(amps, 16 * k, 2) if k else amps
    group = iota((16, 128), 1) // 16
    for peer in range(8):
        block = jnp.zeros((16, 128), F32)
        for c in range(8):
            block = jnp.where(group == c, roll_ref[(c - peer) % 8, :, c, :], block)
        out_ref[peer, 8 * SL : 8 * SL + 16, :] = block


def fold_ov(vir_s, occ_s, aux_ref, c_ref, t_ref, ch_ref, sw_ref, pick_ref, fits_ref):
    o, v = occ_at(), vir_at()
    rows = aux_blocks(aux_ref)
    over = jnp.zeros((8, 1), F32)
    for g in range(NG):
        count = jnp.sum((rows == g).astype(F32), axis=1, keepdims=True)
        over = jnp.maximum(over, jnp.maximum(count - SL, jnp.sum(count, axis=0, keepdims=True) - SG))
    fits_ref[0] = (jnp.max(over) < 0.5).astype(jnp.int32)
    aux = jnp.concatenate([aux_ref[n : n + 1, :] for n in range(6)], axis=1)
    member = (aux == iota((NG, 768), 0)).astype(F32)
    before = (iota((768, 768), 0) < iota((768, 768), 1)).astype(F32).astype(BF16)
    rank = jnp.sum(member * dot(member.astype(BF16), before), axis=0, keepdims=True)
    pick = (rank == iota((SG, 768), 0).astype(F32)).astype(F32).astype(BF16)
    pick_ref[...] = pick
    c_label = jnp.zeros((8, 1), jnp.int32)
    for c in range(8):
        c_label = jnp.where(iota((8, 1), 0) == c, vir_s[v * 8 + c], c_label)
    for k in range(4):
        keep = (c_label ^ occ_s[o * 4 + k]) == aux
        hi, lo = split(jnp.where(keep, c_ref[k], 0.0))
        ch_ref[8 * k : 8 * k + 8, :] = dot_t(hi, pick) + dot_t(lo, pick)
    sw_ref[...] = jnp.transpose(t_ref[...].reshape(128, 128))


def place(aux_ref, place_ref):
    lane = iota((SL, 128), 1).astype(F32) - iota((SL, 128), 0).astype(F32)
    aux = aux_blocks(aux_ref)
    for g in range(NG):
        count = jnp.sum((aux == g).astype(F32), axis=1, keepdims=True)
        start = jnp.zeros((1, 1), F32)
        for block in range(8):
            row = g * 256 + block * SL
            place_ref[row : row + SL, :] = (lane == start).astype(F32)
            start = start + count[block : block + 1, :]
        place_ref[g * 256 + 8 * SL : (g + 1) * 256, :] = jnp.zeros((256 - 8 * SL, 128), F32)


def refold_own(vir_s, aux_ref, vir_ref, r1_ref, ch_ref, sw_ref, out_ref, place_ref, row_ref):
    o, v = occ_at(), vir_at()
    place(aux_ref, place_ref)
    group = iota((1, 128), 1) // 16
    y_row = jnp.broadcast_to(vir_ref[...], (8, 128))
    mine = jnp.zeros((8 * SL, 128), F32)
    label = jnp.zeros((8, 128), jnp.int32)
    for x in range(8):
        shift = lax.rem(16 * x + 128 - 16 * o, 128)
        block = jnp.concatenate([r1_ref[p, x * SL : (x + 1) * SL, :] for p in range(8)], axis=0)
        mine = jnp.where(group == x, pltpu.roll(block, shift, 1), mine)
        label = jnp.where(group == x, pltpu.roll(y_row, shift, 1) ^ vir_s[v * 8 + x], label)
    mine = jnp.transpose(jnp.concatenate([mine, jnp.zeros((256 - 8 * SL, 128), F32)], axis=0))
    label = jnp.transpose(jnp.broadcast_to(label[0:1], (128, 128)))
    label = jnp.concatenate([label, label], axis=1)
    hi, lo = split(mine)
    hi, lo = hi.astype(F32), lo.astype(F32)
    total = jnp.zeros((256, 128), F32)
    for g in range(NG):
        both = jnp.concatenate([jnp.where(label == g, hi, 0.0), jnp.where(label == g, lo, 0.0)], axis=0)
        total = total + dot(both.astype(BF16), place_ref[g * 256 : (g + 1) * 256, :].astype(BF16))
    row_ref[0] = total[:128] + total[128:]
    row_ref[1] = jnp.transpose(
        jnp.concatenate([r1_ref[p, 8 * SL : 8 * SL + 16, :] for p in range(8)], axis=0)
    )
    for d in range(16):
        own = row_ref[0, pl.ds(d, 8, stride=16), :]
        amps = row_ref[1, pl.ds(d, 8, stride=16), :]
        for peer in range(8):
            out_ref[peer, d * 8 : d * 8 + 8, :] = own
            out_ref[peer, 128 + d * 8 : 136 + d * 8, :] = amps
    for peer in range(8):
        out_ref[peer, 256:288, :] = ch_ref[...]
        out_ref[peer, 288:304, :] = sw_ref[16 * peer : 16 * peer + 16, :]


def refold_rows(vir_s, aux_ref, vir_ref, r1_ref, out_ref, place_ref):
    v = vir_at()
    place(aux_ref, place_ref)
    spread = jnp.concatenate(
        [jnp.transpose(place_ref[128 * n : 128 * n + 128, :]).astype(BF16) for n in range(2 * NG)], axis=1
    )
    y_row = vir_ref[...]
    pad = jnp.zeros((256 - 8 * SL, 128), F32)
    for x in range(8):
        label = y_row ^ vir_s[v * 8 + x]
        block = jnp.concatenate([r1_ref[p, x * SL : (x + 1) * SL, :] for p in range(8)] + [pad], axis=0)
        hi, lo = split(block)
        both = jnp.concatenate([hi, lo], axis=1)
        total = jnp.zeros((SG, 256), F32)
        for g in range(NG):
            keep = (label == g).astype(F32)
            keep = jnp.concatenate([keep, keep], axis=1).astype(BF16)
            total = total + dot(spread[:, g * 256 : (g + 1) * 256], both * keep)
        hi, lo = split(total[:, :128] + total[:, 128:])
        out_ref[0:128, x * 128 : x * 128 + 128] = hi
        out_ref[128:256, x * 128 : x * 128 + 128] = lo
        out_ref[256:384, x * 128 : x * 128 + 128] = hi


def cycle_first(occ_s, vir_ref, r2_ref, o2_ref, t_ref, pick_ref, aux_ref, y_ref, chat_ref, f_ref, amps_ref, got_ref):
    o, core = occ_at(), lax.axis_index("core")
    for ref, part in ((r2_ref, core), (o2_ref, 1 - core)):
        for p in range(8):
            f_ref[:, 2 * p + part] = ref[p, 0:128, :].reshape(16, 8, 128)
            amps_ref[:, 2 * p + part] = ref[p, 128:256, :].reshape(16, 8, 128)
    for p in range(8):
        got_ref[2 * p + core] = r2_ref[p, 256:304, :]
        got_ref[2 * p + 1 - core] = o2_ref[p, 256:304, :]
    for k in range(4):
        for n in range(16):
            chat_ref[k * 128 + n * 8 : k * 128 + n * 8 + 8, :] = got_ref[n, 8 * k : 8 * k + 8, :]
    group = iota((8, 128), 1) // 8
    blocks = [got_ref[n, pl.ds(pl.multiple_of(32 + 8 * core, 8), 8), :] for n in range(16)]
    u = []
    for i in range(4):
        row = []
        for k in range(4):
            swapped = jnp.zeros((8, 128), F32)
            for n in range(16):
                shift = (8 * (n - 4 * i - k)) % 128
                swapped = jnp.where(group == n, pltpu.roll(blocks[n], shift, 1) if shift else blocks[n], swapped)
            row.append(2.0 * t_ref[i, k] - swapped)
        u.append(jnp.concatenate(row, axis=1))
    u = jnp.concatenate(u, axis=0)
    label = jnp.concatenate([vir_ref[...] ^ occ_s[o * 4 + k] for k in range(4)], axis=1)
    rows = jnp.concatenate([jnp.where(label == g, u, 0.0) for g in range(NG)], axis=0)
    hi, lo = split(dot3(rows, chat_ref[...], dot))
    y = dot(hi, pick_ref[...]) + dot(lo, pick_ref[...])
    for n in range(6):
        aux = aux_ref[n : n + 1, :]
        part = jnp.zeros((32, 128), F32)
        for g in range(NG):
            part = jnp.where(aux == g, y[32 * g : 32 * g + 32, 128 * n : 128 * n + 128], part)
        y_ref[32 * n : 32 * n + 32, :] = part


def ladder(vir_s, vir_ref, b1_ref, f_ref, t_ref, y_ref, out_ref, hi_ref, lo_ref, acc_ref):
    o, v = occ_at(), vir_at()
    acc_ref[...] = jnp.zeros_like(acc_ref)
    c_lane = jnp.broadcast_to(vir_ref[...], (128, 128))
    bc = jnp.transpose(c_lane) ^ c_lane

    def step(n, carry):
        amps = []
        for half in range(2):
            d = 2 * n + half
            hi, lo = split(f_ref[d].reshape(128, 128))
            w = dot(jnp.concatenate([hi, hi, lo], axis=1), b1_ref[...])
            d_label = vir_s[o * 16 + d]
            for a in range(8):
                keep = bc == (vir_s[v * 8 + a] ^ d_label)
                hi, lo = split(jnp.where(keep, w[:, a * 128 : a * 128 + 128], 0.0))
                hi_ref[a * 128 : a * 128 + 128, half * 128 : half * 128 + 128] = hi
                lo_ref[a * 128 : a * 128 + 128, half * 128 : half * 128 + 128] = lo
            amps.append(t_ref[d].reshape(128, 128))
        hi, lo = split(jnp.concatenate(amps, axis=0))
        r = dot(hi_ref[...], jnp.concatenate([hi, lo], axis=1))
        acc_ref[...] += r[:, :128] + r[:, 128:] + dot(lo_ref[...], hi)
        return carry

    lax.fori_loop(0, 8, step, 0, unroll=True)
    for a in range(8):
        rows = jnp.transpose(acc_ref[a * 128 : a * 128 + 128, :])
        for p in range(8):
            out_ref[p, 16 * a : 16 * a + 16, :] = rows[16 * p : 16 * p + 16, :]
    for p in range(8):
        out_ref[p, 128:320, :] = y_ref[...]


def cycle_and_ladder(
    vir_s, occ_s, vir_ref, aux_ref, r2_ref, o2_ref, t_ref, pick_ref, b1_ref, out_ref, chat_ref,
    y_ref, f_ref, amps_ref, got_ref, hi_ref, lo_ref, acc_ref,
):
    cycle_first(occ_s, vir_ref, r2_ref, o2_ref, t_ref, pick_ref, aux_ref, y_ref, chat_ref, f_ref, amps_ref, got_ref)
    ladder(vir_s, vir_ref, b1_ref, f_ref, amps_ref, y_ref, out_ref, hi_ref, lo_ref, acc_ref)


def unfold(occ_s, vir_ref, chat_ref, pick_ref, aux_ref, hi_ref, lo_ref):
    o = occ_at()
    aux = jnp.concatenate([aux_ref[n : n + 1, :] for n in range(6)], axis=1)
    label = jnp.transpose(jnp.broadcast_to(vir_ref[...], (128, 128)))[:, :1]
    for j in range(4):
        hi, lo = split(chat_ref[128 * j : 128 * j + 128, :])
        wide = dot(hi, pick_ref[...]) + dot(lo, pick_ref[...])
        hi, lo = split(jnp.where((label ^ occ_s[o * 4 + j]) == aux, wide, 0.0))
        hi_ref[128 * j : 128 * j + 128, :] = hi
        lo_ref[128 * j : 128 * j + 128, :] = lo


def finish(r3_ref, ch_ref, cl_ref, out_ref, sum_ref):
    total = r3_ref[0]
    for p in range(1, 8):
        total = total + r3_ref[p]
    sum_ref[...] = total[0:128]
    hi, lo = split(jnp.concatenate([total[128 + 32 * n : 160 + 32 * n] for n in range(6)], axis=1))
    z = dot_t(hi, ch_ref[...]) + dot_t(hi, cl_ref[...]) + dot_t(lo, ch_ref[...])
    for i in range(4):
        for j in range(4):
            part = z[8 * i : 8 * i + 8, 128 * j : 128 * j + 128]
            out_ref[i, j] = sum_ref[pl.ds(i * 4 + j, 8, stride=16), :] + part


def swap(x, axes):
    return lax.all_to_all(x, axes, 0, 0, tiled=True)


def folded(t, b, c, occ, vir, aux):
    aux, row = aux.reshape(6, 128), vir.reshape(1, 128)
    shape = jax.ShapeDtypeStruct
    p1 = call(
        fold_local, shape((8, 8 * SL + 16, 128), F32), 1, 4, [pltpu.VMEM((8, 16, 8, 128), F32)],
        (2 * 2 * 24 * 96 * 1024, 1300000), 56 * 2**20,
    )(vir, aux, row, b, t)
    r1 = swap(p1, OCC)
    ch, sw, pick, fits = pl.pallas_call(
        fold_ov,
        out_shape=(shape((32, 128), F32), shape((128, 128), F32), shape((SG, 768), BF16), shape((1,), jnp.int32)),
        in_specs=[SMEM, SMEM, VMEM, VMEM, VMEM],
        out_specs=(VMEM, VMEM, VMEM, SMEM),
        compiler_params=pltpu.CompilerParams(vmem_limit_bytes=LIMIT),
        cost_estimate=pl.CostEstimate(flops=2 * 8 * 768 * 768, bytes_accessed=300000, transcendentals=0),
    )(vir, occ, aux, jnp.transpose(c, (1, 2, 0)), t)
    p2 = call(
        refold_own, shape((8, 304, 128), F32), 1, 5, [pltpu.VMEM((2048, 128), F32), pltpu.VMEM((2, 128, 128), F32)],
        (2 * 256 * 2048 * 128, 2300000),
    )(vir, aux, row, r1, ch, sw)
    r2 = swap(p2, ZY)
    b1 = call(
        refold_rows, shape((384, 1024), BF16), 1, 3, [pltpu.VMEM((2048, 128), F32)], (2 * 128 * 2048 * 2048, 1700000)
    )(vir, aux, row, r1)
    o2 = lax.ppermute(r2, "core", [(0, 1), (1, 0)])
    staged = (16, 16, 8, 128)
    p3, chat = call(
        cycle_and_ladder, (shape((8, 320, 128), F32), shape((512, 128), F32)), 2, 7,
        [
            pltpu.VMEM((192, 128), F32),
            pltpu.VMEM(staged, F32),
            pltpu.VMEM(staged, F32),
            pltpu.VMEM((16, 48, 128), F32),
            pltpu.VMEM((1024, 256), BF16),
            pltpu.VMEM((1024, 256), BF16),
            pltpu.VMEM((1024, 128), F32),
        ],
        (6 * 2048 * 1024 * 256 + 6 * 2 * 256 * 512 * 128, 5000000),
    )(vir, occ, row, aux, r2, o2, t, pick, b1)
    r3 = swap(p3, OCC)
    ch, cl = call(
        unfold, (shape((512, 768), BF16), shape((512, 768), BF16)), 1, 4, (), (4 * 512 * 768 * 128, 2000000)
    )(occ, row, chat, pick, aux)
    out = call(
        finish, shape((4, 4, 8, 128), F32), 0, 3, [pltpu.VMEM((128, 128), F32)], (6 * 32 * 512 * 768, 3000000)
    )(r3, ch, cl)
    return out, fits


def allowed(left, right, target):
    return (jnp.bitwise_xor(left, right) == target).astype(F32)


def gather(x, axes, n, dim):
    parts = swap(jnp.broadcast_to(x[None], (n,) + x.shape), axes)
    return jnp.concatenate([parts[p] for p in range(n)], axis=dim)


def dense(t, b, c, occ, vir, aux):
    o, v = occ_at(), vir_at()
    aux_mine = lax.dynamic_slice_in_dim(aux, o * 96, 96)
    vir_mine = lax.dynamic_slice_in_dim(vir, v * 8, 8)
    occ_mine = lax.dynamic_slice_in_dim(occ, o * 4, 4)
    own = b * allowed(vir_mine[None, :, None], vir[None, None, :], aux_mine[:, None, None])
    wide = gather(b, VIR, 16, 1)
    wide = wide * allowed(vir[None, :, None], vir[None, None, :], aux_mine[:, None, None])
    pairs = gather(t, OCC, 8, 1)
    inter = jnp.einsum("qac,qbd->acbd", own, wide, precision=HIGHEST)
    part = jnp.einsum("ijcd,acbd->ijab", gather(pairs, VIR, 16, 2), inter, precision=HIGHEST)
    total = jnp.sum(swap(jnp.moveaxis(part.reshape(4, 8, 4, 8, 128), 1, 0), OCC), axis=0)
    swapped = lax.all_to_all(t, VIR, split_axis=3, concat_axis=2, tiled=True)
    u = 2.0 * t - jnp.transpose(swapped, (0, 1, 3, 2))
    cw = gather(c, VIR, 16, 2)
    cw = cw * allowed(occ_mine[None, :, None], vir[None, None, :], aux[:, None, None])
    part = jnp.einsum("ikac,qkc->iaq", u, cw, precision=HIGHEST)
    y = jnp.sum(swap(jnp.broadcast_to(part[None], (8,) + part.shape), OCC), axis=0)
    return total + jnp.einsum("iaq,qjb->ijab", y, cw, precision=HIGHEST)


def shards(t, b, c, occ, vir, aux):
    fast, fits = folded(t, b, c, occ, vir, aux)
    return lax.cond(fits[0] > 0, lambda *_: fast, dense, t, b, c, occ, vir, aux)


def solution(mesh):
    fine = Mesh(mesh.devices.reshape(2, 4, 4, 2, 2), ("yh", "x", "z", "yl", "core"))
    placed = (P(None, OCC, VIR, None), P(OCC, VIR, None), P(None, OCC, VIR), P(), P(), P())
    return jax.shard_map(shards, mesh=fine, in_specs=placed, out_specs=P(None, OCC, VIR, None), check_vma=False)
```
